128 devices in a mesh: blk: 32 (over y, z_lo, x), rep: 4 (over z_hi, core).
Axes of the slice: x: 4, y: 4, z: 4 (z_hi: 2, z_lo: 2; z = z_hi * 2 + z_lo), core: 2. Of those that a mesh axis runs over, the one named last changes fastest.
Arguments:
- loads: bfloat16 [24576, 512], P('blk', 'rep'), may hold values from -6 to 6
- values: bfloat16 [9216, 192, 192], P('blk'), may hold values from -0.0390625 to 0.0390625
- row_ptr: int32 [32, 5], P('blk'), may hold values from 0 to 288, as said below
- col_idx: int32 [9216], P('blk'), may hold values from 0 to 127
- elem_vals: bfloat16 [4096, 192, 192], P(('blk', 'rep')), may hold values from -0.0390625 to 0.0390625
- elem_owner: int32 [4096, 1], P(('blk', 'rep')), may hold values from 0 to 31; in each aligned block of 32 rows (0 to 31, 32 to 63, ...) at most 2 rows name the same one
- elem_row: int32 [4096], P(('blk', 'rep')), may hold values from 0 to 3
- elem_col: int32 [4096], P(('blk', 'rep')), may hold values from 0 to 127
Outputs:
- response: float32 [24576, 512], P('blk', 'rep')
The draws below stay inside these ranges and needn't reach their ends.
Inputs may be any that keep to these rules, and one draw needn't show every extreme that they name: Pointers don't fall along a row; each block row holds 36 to 72 slots; row_ptr[b, 0] = 0, and on some index of blk the last pointer is 288. `elem_owner`: among the 32 elements of one device, no owner is named more than 2 times, a bound that some block reaches.
All inputs are finite; a program needn't handle non-finite values.
Results may differ from the reference program's by a relative error of at most 0.0029.
Values may be sent and summed in bfloat16 or wider, within the bound.
A program may use at most 192 MiB of HBM per device.

```python
import math
import jax
import jax.numpy as jnp
import numpy as np
from jax import lax

BS = 192
BR_DEV = 4
NNZ_DEV = 288
E_DEV = 32
NBC = 128
NROWS = 24576
NCASE = 512
CAP = 2
ELEMS = 4096
N_BLK = 32


def draw_row_ptr(key, part):
    key = jax.random.fold_in(key, 11)
    first, second = jax.random.split(key)
    lower = NNZ_DEV // (2 * BR_DEV)
    upper = NNZ_DEV // BR_DEV
    device_count = NBC // BR_DEV
    lengths = jax.random.randint(first, (device_count, BR_DEV), lower, upper + 1)
    chosen = jax.random.randint(second, (), 0, device_count)
    lengths = jnp.where(jnp.arange(device_count)[:, None] == chosen, upper, lengths)
    starts = jnp.zeros((device_count, 1), jnp.int32)
    return jnp.concatenate([starts, jnp.cumsum(lengths, axis=1).astype(jnp.int32)], axis=1)


def set_ends(values, key, smallest, high):
    shape = values.shape
    place = [jax.random.randint(jax.random.fold_in(key, axis), (), 0, shape[axis]) for axis in range(len(shape))]
    values = values.at[tuple(place)].set(smallest)
    longest = shape.index(max(shape))
    place[longest] = (place[longest] + 1) % shape[longest]
    return values.at[tuple(place)].set(high)


def block_levels(stream_key, shape, shards, least, high):
    level = 1.0
    for axis_at, blocks in shards:
        steps = jax.random.uniform(jax.random.fold_in(jax.random.fold_in(stream_key, 6), axis_at), (blocks,), jnp.float32, least / len(shards), high / len(shards))
        level = level * jnp.repeat(jnp.exp(steps), shape[axis_at] // blocks).reshape((-1,) + (1,) * (len(shape) - 1 - axis_at))
    return level


def assign_block(rng, own, number, rows, number_of, top, bound, lean):
    sequence = jax.random.permutation(rng, number_of)
    crowded, common = shares(number_of, rows * top, bound, lean, True), shares(number_of, rows * top, bound, lean, False)
    places = jnp.arange(number_of)

    def named(sizes, offset_by):
        used = int((sizes > 0).sum())
        fixed = max(1, used // 4)
        passed = fixed + (places - fixed + offset_by * (used - fixed)) % max(1, number_of - fixed)
        return jnp.zeros((number_of,), jnp.int32).at[sequence[jnp.where(places < fixed, places, passed)]].set(jnp.asarray(sizes, jnp.int32))

    sizes = jnp.where(number % 4 == 0, named(crowded, number // 4), named(common, number - number // 4 - 1))
    mixed = jax.random.permutation(jax.random.fold_in(own, 3), number_of)
    giver, receiver = mixed[0:number_of // 2 * 2:2], mixed[1:number_of // 2 * 2:2]
    margin = jnp.minimum(sizes[giver] - 1, bound - sizes[receiver]) // 2
    margin = jnp.where((giver == sequence[0]) | (receiver == sequence[0]) | (sizes[receiver] == 0), 0, jnp.maximum(margin, 0))
    passed = jax.random.randint(jax.random.fold_in(own, 4), (number_of // 2,), 0, 1 << 20) % (margin + 1)
    sizes = sizes.at[giver].add(-passed).at[receiver].add(passed)
    labels = jnp.searchsorted(jnp.cumsum(sizes), jnp.arange(rows * top), side="right").astype(jnp.int32)
    table = labels.reshape(top, rows).T
    table = table[jax.random.permutation(jax.random.fold_in(own, 1), rows)]
    offset_by = jax.random.randint(jax.random.fold_in(own, 2), (rows, 1), 0, top)
    return jnp.take_along_axis(table, (jnp.arange(top)[None, :] + offset_by) % top, axis=1)


def shares(number_of, total, most, slope, full):
    weights = [(1 << 20) // math.isqrt(grade ** slope) + 1 for grade in range(1, number_of + 1)]
    largest = most if full else min(most, max(-(-total // number_of), total * weights[0] // sum(weights)))
    least = 1 if total - largest >= number_of - 1 else 0
    given, rest = [largest] + [least] * (number_of - 1), total - largest - least * (number_of - 1)
    while rest > 0:
        movable = [i for i in range(1, number_of) if given[i] < largest] or [i for i in range(1, number_of) if given[i] < most]
        pool, budget = sum([weights[i] for i in movable]), rest
        for i in movable:
            extra = min(most - given[i], max(1, budget * weights[i] // pool), rest)
            given[i] = given[i] + extra
            rest = rest - extra
    return np.array(given)


def normal_values(own_key, dims, deviation, most, cuts=(), held_as=jnp.bfloat16):
    drawn = jax.random.normal(own_key, dims, jnp.float32) * deviation
    if len(cuts) > 0:
        drawn = block_levels(own_key, dims, cuts, -0.22, 0.18) * drawn
    return jnp.clip(drawn, min=-most, max=most).astype(held_as)


def setup_inputs(seed: int = 0) -> dict:
    keys = jax.random.split(jax.random.key(seed), 9)
    loads = normal_values(keys[0], (NROWS, NCASE), 1.0, 6.0, ((0, 32), (1, 4)))
    values = normal_values(keys[1], (N_BLK * NNZ_DEV, BS, BS), (BS * (NNZ_DEV + 4 * E_DEV) // BR_DEV) ** -0.5, 0.0390625, ((0, 32),))
    row_ptr = draw_row_ptr(jax.random.fold_in(keys[8], 71), 0)
    col_idx = set_ends(jax.random.randint(keys[3], (N_BLK * NNZ_DEV,), 0, NBC), jax.random.fold_in(keys[3], 1), 0, NBC - 1).astype(jnp.int32)
    elem_vals = normal_values(keys[4], (ELEMS, BS, BS), (BS * (NNZ_DEV + 4 * E_DEV) // BR_DEV) ** -0.5, 0.0390625, ((0, 128),))
    elem_owner_keys = jax.random.split(jax.random.fold_in(keys[5], 1), ELEMS // E_DEV)
    elem_owner_turns = jax.random.permutation(jax.random.fold_in(keys[5], 3), ELEMS // E_DEV)
    elem_owner = jax.vmap(lambda own, number: assign_block(jax.random.fold_in(keys[5], 2), own, number, E_DEV, N_BLK, 1, CAP, 2))(elem_owner_keys, elem_owner_turns).reshape((ELEMS, 1))
    elem_row = set_ends(jax.random.randint(keys[6], (ELEMS,), 0, BR_DEV), jax.random.fold_in(keys[6], 1), 0, BR_DEV - 1).astype(jnp.int32)
    elem_col = set_ends(jax.random.randint(keys[7], (ELEMS,), 0, NBC), jax.random.fold_in(keys[7], 1), 0, NBC - 1).astype(jnp.int32)
    return dict(loads=loads, values=values, row_ptr=row_ptr, col_idx=col_idx, elem_vals=elem_vals, elem_owner=elem_owner, elem_row=elem_row, elem_col=elem_col)


def apply_matrix(panel, values, row_ptr, col_idx, elem_vals, elem_owner, elem_row, elem_col):
    case_cols = panel.shape[1]
    blocks = panel.reshape(NBC, BS, case_cols).astype(jnp.float32)
    device_count = NBC // BR_DEV
    positions = jnp.arange(NNZ_DEV, dtype=jnp.int32)

    def slot_advance(total, pieces):
        block_set, columns, pointers, device = pieces
        row_of_slot = jnp.sum((positions[:, None] >= pointers[None, 1:]).astype(jnp.int32), axis=1)
        live_mask = (row_of_slot < BR_DEV).astype(jnp.float32)
        target = device * BR_DEV + jnp.minimum(row_of_slot, BR_DEV - 1)
        products = jnp.einsum("gij,gjc->gic", block_set.astype(jnp.float32), blocks[columns])
        return total.at[target].add(products * live_mask[:, None, None]), None

    start_total = jnp.zeros((NBC, BS, case_cols), jnp.float32)
    total, _ = lax.scan(slot_advance, start_total, (values.reshape(device_count, NNZ_DEV, BS, BS), col_idx.reshape(device_count, NNZ_DEV), row_ptr, jnp.arange(device_count, dtype=jnp.int32)))

    group_count = ELEMS // E_DEV
    elem_target = (elem_owner[:, 0] * BR_DEV + elem_row).astype(jnp.int32)

    def elem_advance(total, pieces):
        block_set, columns, target = pieces
        products = jnp.einsum("gij,gjc->gic", block_set.astype(jnp.float32), blocks[columns])
        return total.at[target].add(products), None

    total, _ = lax.scan(elem_advance, total, (elem_vals.reshape(group_count, E_DEV, BS, BS), elem_col.reshape(group_count, E_DEV), elem_target.reshape(group_count, E_DEV)))
    return total.reshape(NBC * BS, case_cols)


def reference(loads, values, row_ptr, col_idx, elem_vals, elem_owner, elem_row, elem_col):
    first = apply_matrix(loads, values, row_ptr, col_idx, elem_vals, elem_owner, elem_row, elem_col).astype(jnp.bfloat16)
    return apply_matrix(first, values, row_ptr, col_idx, elem_vals, elem_owner, elem_row, elem_col)
```

```python
import functools

import jax
import jax.numpy as jnp
from jax import lax
from jax.experimental import pallas as pl
from jax.experimental.pallas import tpu as pltpu
from jax.sharding import PartitionSpec as P

MESH = pl.DeviceIdType.MESH
BS = 192
ROWS = 768
LANES = 128
PACKED = 288
CHUNK = 16
DEPTH = 4


class Place:
    def __init__(self):
        blk = lax.axis_index("blk")
        rep = lax.axis_index("rep")
        self.x = lax.rem(blk, 4)
        self.zl = lax.rem(blk // 4, 2)
        self.y = blk // 8
        self.zh = rep // 2
        self.core = lax.rem(rep, 2)

    def block(self, dx, dy, dz):
        x = lax.rem(self.x + dx, 4)
        y = lax.rem(self.y + dy, 4)
        zl = lax.rem(self.zl + dz, 2)
        return (y * 2 + zl) * 4 + x

    def device(self, dx, dy, dz, dzh=0, dcore=0):
        zh = lax.rem(self.zh + dzh, 2)
        core = lax.rem(self.core + dcore, 2)
        return (self.block(dx, dy, dz), zh * 2 + core)


def wait_bytes(ref, sem):
    pltpu.make_async_copy(ref, ref, sem).wait()


class Gather:
    def __init__(self, place, g, sems):
        self.place = place
        self.g = g
        self.sends, self.cross_s, self.cross_r, self.sem_z, self.sem1, self.sem1f, self.sem2, self.sem2f = sems
        self.lanes = pl.ds(pl.multiple_of(place.core * LANES, LANES), LANES)
        self.other = pl.ds(pl.multiple_of((1 - place.core) * LANES, LANES), LANES)

    def peers(self):
        p = self.place
        return [
            p.device(0, 0, 1),
            p.device(1, 0, 0),
            p.device(3, 0, 0),
            p.device(0, 1, 0),
            p.device(0, 3, 0),
            p.device(0, 0, 0, 0, 1),
        ]

    def piece(self, half, p1, p2, dz, start=0, size=384):
        block = self.place.block(p1, p2, dz) if half == 0 else self.place.block(p2, p1, dz)
        first = pl.multiple_of(block * ROWS + (half * 384 + start), BS)
        return self.g.at[pl.ds(first, size), self.lanes]

    def peer(self, half, stage, step):
        along_x = (half == 0) == (stage == 1)
        return self.place.device(step, 0, 0) if along_x else self.place.device(0, step, 0)

    def send(self, ref, device, sem):
        pltpu.make_async_remote_copy(ref, ref, self.sends, sem, device_id=device, device_id_type=MESH).start()

    def cross(self, ref):
        pltpu.make_async_remote_copy(
            ref, ref, self.cross_s, self.cross_r, device_id=self.place.device(0, 0, 0, 0, 1), device_id_type=MESH
        ).start()

    def chunk(self, dz):
        first = pl.multiple_of(self.place.block(0, 0, dz) * ROWS, ROWS)
        return self.g.at[pl.ds(first, ROWS), self.lanes]

    def start(self):
        self.send(self.chunk(0), self.place.device(0, 0, 1), self.sem_z)
        self.spread1(0)
        self.spread2(0, 0, 0, 0)
        self.spread2(1, 0, 0, 0)
        self.cross(self.chunk(0))

    def spread1(self, dz):
        for half in (0, 1):
            for way in (0, 1):
                self.send(
                    self.piece(half, 0, 0, dz), self.peer(half, 1, 1 if way == 0 else 3), self.sem1.at[half, dz, way]
                )

    def spread2(self, half, k, p1, dz):
        for way in (0, 1):
            self.send(
                self.piece(half, p1, 0, dz), self.peer(half, 2, 1 if way == 0 else 3), self.sem2.at[half, k, way]
            )

    def neighbour_z(self):
        wait_bytes(self.chunk(1), self.sem_z)
        self.spread1(1)
        self.spread2(0, 1, 0, 1)
        self.spread2(1, 1, 0, 1)
        self.cross(self.chunk(1))

    def pass1(self, dz):
        for half in (0, 1):
            for way in (0, 1):
                p1 = 3 if way == 0 else 1
                got = self.piece(half, p1, 0, dz)
                wait_bytes(got, self.sem1.at[half, dz, way])
                self.send(
                    self.piece(half, p1, 0, dz, way * BS, BS),
                    self.peer(half, 1, 1 if way == 0 else 3),
                    self.sem1f.at[half, dz, way],
                )
                k = (4 if p1 == 3 else 2) + dz
                self.spread2(half, k, p1, dz)
                self.cross(got)

    def far1(self, dz):
        for half in (0, 1):
            for way in (0, 1):
                wait_bytes(self.piece(half, 2, 0, dz, way * BS, BS), self.sem1f.at[half, dz, way])
            self.spread2(half, 6 + dz, 2, dz)
            self.cross(self.piece(half, 2, 0, dz))

    def pass2(self, k):
        q = k // 2
        p1, dz = q ^ (q // 2), lax.rem(k, 2)
        for half in (0, 1):
            for way in (0, 1):
                p2 = 3 if way == 0 else 1
                got = self.piece(half, p1, p2, dz)
                wait_bytes(got, self.sem2.at[half, k, way])
                self.send(
                    self.piece(half, p1, p2, dz, way * BS, BS),
                    self.peer(half, 2, 1 if way == 0 else 3),
                    self.sem2f.at[half, k, way],
                )
                self.cross(got)

    def far2(self, k):
        q = k // 2
        p1, dz = q ^ (q // 2), lax.rem(k, 2)
        for half in (0, 1):
            for way in (0, 1):
                wait_bytes(self.piece(half, p1, 2, dz, way * BS, BS), self.sem2f.at[half, k, way])
            self.cross(self.piece(half, p1, 2, dz))

    def finish(self):
        wait_bytes(self.g.at[:, self.other], self.cross_r)
        wait_bytes(self.g.at[:, self.lanes], self.cross_s)
        wait_bytes(self.g.at[pl.ds(0, 31 * ROWS), self.lanes], self.sends)


def gather_scratch():
    dma = pltpu.SemaphoreType.DMA
    return [dma, dma, dma, dma, dma((2, 2, 2)), dma((2, 2, 2)), dma((2, 8, 2)), dma((2, 8, 2))]


def greet(devices):
    barrier = pltpu.get_barrier_semaphore()
    for device in devices:
        pl.semaphore_signal(barrier, inc=1, device_id=device, device_id_type=MESH)
    return barrier


def exchange_kernel(loads, elems, places, codes, g, r, m, packed, es, er, ms, mr, own, *sems):
    place = Place()
    gather = Gather(place, g, sems)
    me = place.block(0, 0, 0)
    barrier = greet(gather.peers())

    def greet_step(t, _):
        dx, dy, dz = lax.rem(t, 4), lax.rem(t // 4, 4), t // 16
        for dzh in (0, 1):
            def say():
                pl.semaphore_signal(
                    barrier, inc=1, device_id=place.device(dx, dy, dz, dzh), device_id_type=MESH
                )
            if dzh == 1:
                say()
            else:
                pl.when(t > 0)(say)
        return 0

    lax.fori_loop(0, 32, greet_step, 0)
    mine = pltpu.make_async_copy(loads, gather.chunk(0), own)
    mine.start()
    mine.wait()
    pl.semaphore_wait(barrier, 6 + 63)
    gather.start()
    where = place.zh * 32 + me

    def element_step(t):
        dx, dy, dz = lax.rem(t, 4), lax.rem(t // 4, 4), t // 16
        target = place.block(dx, dy, dz)
        for k in (0, 1):
            block = elems[places[target * 2 + k]]
            packed[t, k, pl.ds(0, BS), :] = block[:, :LANES]
            packed[t, k, pl.ds(BS, 96), :] = jnp.concatenate([block[:96, LANES:], block[96:, LANES:]], axis=1)

        def remote(dzh):
            device = place.device(dx, dy, dz, dzh)
            pltpu.make_async_remote_copy(
                packed.at[t], r.at[where], es, er, device_id=device, device_id_type=MESH
            ).start()
            pltpu.make_async_remote_copy(
                codes, m.at[where], ms, mr, device_id=device, device_id_type=MESH
            ).start()

        remote(1)

        @pl.when(t > 0)
        def _():
            remote(0)

        @pl.when(t == 0)
        def _():
            pltpu.make_async_copy(packed.at[t], r.at[where], er).start()
            pltpu.make_async_copy(codes, m.at[where], mr).start()

    def elements(first, last):
        def step(t, _):
            element_step(t)
            return 0

        lax.fori_loop(first, last, step, 0)

    elements(0, 2)
    gather.neighbour_z()
    elements(2, 4)
    gather.pass1(0)
    elements(4, 6)
    gather.pass1(1)
    elements(6, 7)
    gather.far1(0)
    elements(7, 8)
    gather.far1(1)

    def step2(k, _):
        gather.pass2(k)
        element_step(8 + 2 * k)
        element_step(9 + 2 * k)
        return 0

    lax.fori_loop(0, 8, step2, 0)

    def step3(k, _):
        gather.far2(k)
        element_step(24 + k)
        return 0

    lax.fori_loop(0, 8, step3, 0)
    gather.finish()
    wait_bytes(r, er)
    wait_bytes(m, mr)
    wait_bytes(r.at[pl.ds(0, 63)], es)
    wait_bytes(m.at[pl.ds(0, 63)], ms)


def exchange(loads, elems, places, codes):
    any_space = pl.BlockSpec(memory_space=pl.ANY)
    dma = pltpu.SemaphoreType.DMA
    return pl.pallas_call(
        exchange_kernel,
        out_shape=[
            jax.ShapeDtypeStruct((32 * ROWS, 2 * LANES), jnp.bfloat16),
            jax.ShapeDtypeStruct((64, 2, PACKED, LANES), jnp.bfloat16),
            jax.ShapeDtypeStruct((64, 8, LANES), jnp.int32),
        ],
        in_specs=[
            any_space,
            pl.BlockSpec(memory_space=pltpu.VMEM),
            pl.BlockSpec(memory_space=pltpu.SMEM),
            any_space,
        ],
        out_specs=[any_space, any_space, any_space],
        scratch_shapes=[pltpu.VMEM((32, 2, PACKED, LANES), jnp.bfloat16), dma, dma, dma, dma, dma, *gather_scratch()],
        compiler_params=pltpu.CompilerParams(collective_id=1, has_side_effects=True, vmem_limit_bytes=32 << 20),
        name="exchange",
    )(loads, elems, places, codes)


def share_sum(place, part, came, send_sem, recv_sem):
    lanes = pl.ds(pl.multiple_of(place.core * LANES, LANES), LANES)
    other = pl.ds(pl.multiple_of((1 - place.core) * LANES, LANES), LANES)
    copy = pltpu.make_async_remote_copy(
        part.at[:, other], came, send_sem, recv_sem, device_id=place.device(0, 0, 0, 0, 1), device_id_type=MESH
    )
    copy.start()
    copy.wait()
    return part[:, lanes] + came[...]


def gather_kernel(part, g, came, first, send_sem, recv_sem, own, *sems):
    place = Place()
    gather = Gather(place, g, sems)
    barrier = greet(gather.peers())
    pl.semaphore_wait(barrier, 6)
    first[...] = share_sum(place, part, came, send_sem, recv_sem).astype(jnp.bfloat16)
    mine = pltpu.make_async_copy(first, gather.chunk(0), own)
    mine.start()
    mine.wait()
    gather.start()
    gather.neighbour_z()
    gather.pass1(0)
    gather.pass1(1)
    gather.far1(0)
    gather.far1(1)

    def step2(k, _):
        gather.pass2(k)
        return 0

    lax.fori_loop(0, 8, step2, 0)

    def step3(k, _):
        gather.far2(k)
        return 0

    lax.fori_loop(0, 8, step3, 0)
    gather.finish()


def gather_first(part):
    dma = pltpu.SemaphoreType.DMA
    return pl.pallas_call(
        gather_kernel,
        out_shape=jax.ShapeDtypeStruct((32 * ROWS, 2 * LANES), jnp.bfloat16),
        in_specs=[pl.BlockSpec(memory_space=pltpu.VMEM)],
        out_specs=pl.BlockSpec(memory_space=pl.ANY),
        scratch_shapes=[
            pltpu.VMEM((ROWS, LANES), jnp.float32),
            pltpu.VMEM((ROWS, LANES), jnp.bfloat16),
            dma,
            dma,
            dma,
            *gather_scratch(),
        ],
        compiler_params=pltpu.CompilerParams(collective_id=2, has_side_effects=True, vmem_limit_bytes=16 << 20),
        name="gather_first",
    )(part)


def sum_kernel(part, out, came, send_sem, recv_sem):
    place = Place()
    barrier = greet([place.device(0, 0, 0, 0, 1)])
    pl.semaphore_wait(barrier, 1)
    out[...] = share_sum(place, part, came, send_sem, recv_sem)


def sum_cores(part):
    dma = pltpu.SemaphoreType.DMA
    return pl.pallas_call(
        sum_kernel,
        out_shape=jax.ShapeDtypeStruct((ROWS, LANES), jnp.float32),
        in_specs=[pl.BlockSpec(memory_space=pltpu.VMEM)],
        out_specs=pl.BlockSpec(memory_space=pltpu.VMEM),
        scratch_shapes=[pltpu.VMEM((ROWS, LANES), jnp.float32), dma, dma],
        compiler_params=pltpu.CompilerParams(collective_id=3, has_side_effects=True, vmem_limit_bytes=16 << 20),
        name="sum_cores",
    )(part)


def product_kernel(turn, vrow, vcol, erow, ecol, vals, elems, g, out, panel, vbuf, ebuf, acc, psem, vsem, esem):
    v_count = vals.shape[0] // (2 * CHUNK)
    e_count = elems.shape[0] // CHUNK
    core = turn[0]

    def v_copy(j, slot):
        first = (2 * j + core) * CHUNK
        return pltpu.make_async_copy(vals.at[pl.ds(first, CHUNK)], vbuf.at[slot], vsem.at[slot])

    def e_copy(j, slot):
        return pltpu.make_async_copy(elems.at[pl.ds(j * CHUNK, CHUNK)], ebuf.at[slot], esem.at[slot])

    for q in range(8):
        pltpu.make_async_copy(g.at[pl.ds(q * 16, 16)], panel.at[pl.ds(q * 16, 16)], psem.at[q]).start()
    for j in range(DEPTH):
        v_copy(j, j).start()
        e_copy(j, j).start()
    acc[...] = jnp.zeros_like(acc)
    for q in range(8):
        pltpu.make_async_copy(g.at[pl.ds(q * 16, 16)], panel.at[pl.ds(q * 16, 16)], psem.at[q]).wait()

    def v_step(j, _):
        slot = lax.rem(j, DEPTH)
        v_copy(j, slot).wait()
        for u in range(CHUNK):
            s = (2 * j + core) * CHUNK + u
            acc[vrow[s]] += jnp.dot(vbuf[slot, u], panel[vcol[s]], preferred_element_type=jnp.float32)

        @pl.when(j + DEPTH < v_count)
        def _():
            v_copy(j + DEPTH, slot).start()

        return 0

    lax.fori_loop(0, v_count, v_step, 0)

    def e_step(j, _):
        slot = lax.rem(j, DEPTH)
        e_copy(j, slot).wait()
        for u in range(CHUNK):
            s = j * CHUNK + u
            tail = ebuf[slot, u, pl.ds(BS, 96)]
            right = jnp.concatenate([tail[:, :64], tail[:, 64:]], axis=0)
            block = jnp.concatenate([ebuf[slot, u, pl.ds(0, BS)], right], axis=1)
            acc[erow[s]] += jnp.dot(block, panel[ecol[s]], preferred_element_type=jnp.float32)

        @pl.when(j + DEPTH < e_count)
        def _():
            e_copy(j + DEPTH, slot).start()

        return 0

    lax.fori_loop(0, e_count, e_step, 0)
    out[...] = acc[:4].reshape(out.shape)


def products(turn, vrow, vcol, erow, ecol, vals, elems, g):
    smem = pl.BlockSpec(memory_space=pltpu.SMEM)
    any_space = pl.BlockSpec(memory_space=pl.ANY)
    dma = pltpu.SemaphoreType.DMA
    return pl.pallas_call(
        product_kernel,
        out_shape=jax.ShapeDtypeStruct((ROWS, 2 * LANES), jnp.float32),
        in_specs=[smem] * 5 + [any_space] * 3,
        out_specs=pl.BlockSpec(memory_space=pltpu.VMEM),
        scratch_shapes=[
            pltpu.VMEM((128, BS, 2 * LANES), jnp.bfloat16),
            pltpu.VMEM((DEPTH, CHUNK, BS, BS), jnp.bfloat16),
            pltpu.VMEM((DEPTH, CHUNK, PACKED, LANES), jnp.bfloat16),
            pltpu.VMEM((5, BS, 2 * LANES), jnp.float32),
            dma((8,)),
            dma((DEPTH,)),
            dma((DEPTH,)),
        ],
        compiler_params=pltpu.CompilerParams(vmem_limit_bytes=40 << 20),
        name="products",
    )(turn, vrow, vcol, erow, ecol, vals, elems, g.reshape(128, BS, 2 * LANES))


def body(loads, values, row_ptr, col_idx, elem_vals, elem_owner, elem_row, elem_col):
    owners = elem_owner[:, 0]
    count = owners.shape[0]
    order = jnp.arange(count, dtype=jnp.int32)
    earlier = (owners[:, None] == owners[None, :]) & (order[None, :] < order[:, None])
    rank = jnp.sum(earlier.astype(jnp.int32), axis=1)
    slot = owners * 2 + rank
    taken = slot[None, :] == jnp.arange(LANES, dtype=jnp.int32)[:, None]
    places = jnp.sum(jnp.where(taken, order[None, :], 0), axis=1)
    code = jnp.sum(jnp.where(taken, (elem_row * 128 + elem_col + 1)[None, :], 0), axis=1)
    codes = jnp.broadcast_to(code[None, :], (8, LANES))
    g, r, m = exchange(loads, elem_vals, places, codes)

    blk = lax.axis_index("blk")
    core = lax.rem(lax.axis_index("rep"), 2).astype(jnp.int32)
    mine = lax.dynamic_slice(m, (0, 0, blk * 2), (64, 1, 2)).reshape(128) - 1
    erow = jnp.where(mine < 0, 4, mine // 128)
    ecol = jnp.where(mine < 0, 0, lax.rem(mine, 128))
    positions = jnp.arange(values.shape[0], dtype=jnp.int32)
    vrow = jnp.sum((positions[:, None] >= row_ptr[0, 1:][None, :]).astype(jnp.int32), axis=1)
    turn = core.reshape(1)
    apply = functools.partial(products, turn, vrow, col_idx, erow, ecol, values, r.reshape(128, PACKED, LANES))
    part = apply(g)
    g2 = gather_first(part)
    return sum_cores(apply(g2))


def solution(mesh):
    placed = (
        P("blk", "rep"),
        P("blk", None, None),
        P("blk", None),
        P("blk"),
        P(("blk", "rep"), None, None),
        P(("blk", "rep"), None),
        P(("blk", "rep")),
        P(("blk", "rep")),
    )
    return jax.shard_map(body, mesh=mesh, in_specs=placed, out_specs=P("blk", "rep"), check_vma=False)
```

```python
import functools

import jax
import jax.numpy as jnp
from jax import lax
from jax.experimental import pallas as pl
from jax.experimental.pallas import tpu as pltpu
from jax.sharding import PartitionSpec as P

MESH = pl.DeviceIdType.MESH
BS = 192
ROWS = 768
LANES = 128
PACKED = 288
CHUNK = 16
DEPTH = 4


class Place:
    def __init__(self):
        blk = lax.axis_index("blk")
        rep = lax.axis_index("rep")
        self.x = lax.rem(blk, 4)
        self.zl = lax.rem(blk // 4, 2)
        self.y = blk // 8
        self.zh = rep // 2
        self.core = lax.rem(rep, 2)

    def block(self, dx, dy, dz):
        x = lax.rem(self.x + dx, 4)
        y = lax.rem(self.y + dy, 4)
        zl = lax.rem(self.zl + dz, 2)
        return (y * 2 + zl) * 4 + x

    def above(self, dz):
        z = lax.rem(self.zh * 2 + self.zl + dz, 4)
        return ((self.y * 2 + lax.rem(z, 2)) * 4 + self.x, (z // 2) * 2 + self.core)

    def device(self, dx, dy, dz, dzh=0, dcore=0):
        zh = lax.rem(self.zh + dzh, 2)
        core = lax.rem(self.core + dcore, 2)
        return (self.block(dx, dy, dz), zh * 2 + core)


SHIFTS = (
    (0, 0), (2, 2), (1, 1), (3, 3), (1, 3), (3, 1), (2, 1), (2, 3),
    (1, 2), (3, 2), (1, 0), (3, 0), (0, 1), (0, 3), (2, 0), (0, 2),
)


def shift(q):
    dx = dy = 0
    for i, (a, b) in enumerate(SHIFTS):
        dx = jnp.where(q == i, a, dx)
        dy = jnp.where(q == i, b, dy)
    return dx, dy


def wait_bytes(ref, sem):
    pltpu.make_async_copy(ref, ref, sem).wait()


class Gather:
    def __init__(self, place, g, sems):
        self.place = place
        self.g = g
        self.sends, self.cross_s, self.cross_r, self.sem_z, self.sem1, self.sem1f, self.sem2, self.sem2f = sems
        self.lanes = pl.ds(pl.multiple_of(place.core * LANES, LANES), LANES)
        self.other = pl.ds(pl.multiple_of((1 - place.core) * LANES, LANES), LANES)

    def peers(self):
        p = self.place
        return [
            p.device(0, 0, 1),
            p.device(1, 0, 0),
            p.device(3, 0, 0),
            p.device(0, 1, 0),
            p.device(0, 3, 0),
            p.device(0, 0, 0, 0, 1),
        ]

    def piece(self, half, p1, p2, dz, start=0, size=384):
        block = self.place.block(p1, p2, dz) if half == 0 else self.place.block(p2, p1, dz)
        first = pl.multiple_of(block * ROWS + (half * 384 + start), BS)
        return self.g.at[pl.ds(first, size), self.lanes]

    def peer(self, half, stage, step):
        along_x = (half == 0) == (stage == 1)
        return self.place.device(step, 0, 0) if along_x else self.place.device(0, step, 0)

    def send(self, ref, device, sem):
        pltpu.make_async_remote_copy(ref, ref, self.sends, sem, device_id=device, device_id_type=MESH).start()

    def cross(self, ref):
        pltpu.make_async_remote_copy(
            ref, ref, self.cross_s, self.cross_r, device_id=self.place.device(0, 0, 0, 0, 1), device_id_type=MESH
        ).start()

    def chunk(self, dz):
        first = pl.multiple_of(self.place.block(0, 0, dz) * ROWS, ROWS)
        return self.g.at[pl.ds(first, ROWS), self.lanes]

    def start(self):
        self.send(self.chunk(0), self.place.device(0, 0, 1), self.sem_z)
        self.spread1(0)
        self.spread2(0, 0, 0, 0)
        self.spread2(1, 0, 0, 0)
        self.cross(self.chunk(0))

    def spread1(self, dz):
        for half in (0, 1):
            for way in (0, 1):
                self.send(
                    self.piece(half, 0, 0, dz), self.peer(half, 1, 1 if way == 0 else 3), self.sem1.at[half, dz, way]
                )

    def spread2(self, half, k, p1, dz):
        for way in (0, 1):
            self.send(
                self.piece(half, p1, 0, dz), self.peer(half, 2, 1 if way == 0 else 3), self.sem2.at[half, k, way]
            )

    def neighbour_z(self):
        wait_bytes(self.chunk(1), self.sem_z)
        self.spread1(1)
        self.spread2(0, 1, 0, 1)
        self.spread2(1, 1, 0, 1)
        self.cross(self.chunk(1))

    def pass1(self, dz):
        for half in (0, 1):
            for way in (0, 1):
                p1 = 3 if way == 0 else 1
                got = self.piece(half, p1, 0, dz)
                wait_bytes(got, self.sem1.at[half, dz, way])
                self.send(
                    self.piece(half, p1, 0, dz, way * BS, BS),
                    self.peer(half, 1, 1 if way == 0 else 3),
                    self.sem1f.at[half, dz, way],
                )
                k = (4 if p1 == 3 else 2) + dz
                self.spread2(half, k, p1, dz)
                self.cross(got)

    def far1(self, dz):
        for half in (0, 1):
            for way in (0, 1):
                wait_bytes(self.piece(half, 2, 0, dz, way * BS, BS), self.sem1f.at[half, dz, way])
            self.spread2(half, 6 + dz, 2, dz)
            self.cross(self.piece(half, 2, 0, dz))

    def pass2(self, k):
        q = k // 2
        p1, dz = q ^ (q // 2), lax.rem(k, 2)
        for half in (0, 1):
            for way in (0, 1):
                p2 = 3 if way == 0 else 1
                got = self.piece(half, p1, p2, dz)
                wait_bytes(got, self.sem2.at[half, k, way])
                self.send(
                    self.piece(half, p1, p2, dz, way * BS, BS),
                    self.peer(half, 2, 1 if way == 0 else 3),
                    self.sem2f.at[half, k, way],
                )
                self.cross(got)

    def far2(self, k):
        q = k // 2
        p1, dz = q ^ (q // 2), lax.rem(k, 2)
        for half in (0, 1):
            for way in (0, 1):
                wait_bytes(self.piece(half, p1, 2, dz, way * BS, BS), self.sem2f.at[half, k, way])
            self.cross(self.piece(half, p1, 2, dz))

    def finish(self):
        wait_bytes(self.g.at[:, self.other], self.cross_r)
        wait_bytes(self.g.at[:, self.lanes], self.cross_s)
        wait_bytes(self.g.at[pl.ds(0, 31 * ROWS), self.lanes], self.sends)


def gather_scratch():
    dma = pltpu.SemaphoreType.DMA
    return [dma, dma, dma, dma, dma((2, 2, 2)), dma((2, 2, 2)), dma((2, 8, 2)), dma((2, 8, 2))]


def greet(devices):
    barrier = pltpu.get_barrier_semaphore()
    for device in devices:
        pl.semaphore_signal(barrier, inc=1, device_id=device, device_id_type=MESH)
    return barrier


def exchange_kernel(loads, elems, places, codes, g, r, m, t, packed, ed, es, er, ee, eo, ms, mz, mr, mzr, own, *sems):
    place = Place()
    gather = Gather(place, g, sems)
    spot = place.y * 4 + place.x
    level = place.zh * 2 + place.zl
    barrier = greet(gather.peers() + [place.above(dz) for dz in (1, 2, 3)])

    def greet_step(q, _):
        dx, dy = shift(q)
        pl.semaphore_signal(barrier, inc=1, device_id=place.device(dx, dy, 0), device_id_type=MESH)
        return 0

    lax.fori_loop(1, 16, greet_step, 0)
    mine = pltpu.make_async_copy(loads, gather.chunk(0), own)
    mine.start()
    mine.wait()
    pl.semaphore_wait(barrier, 6 + 3 + 15)
    gather.start()

    def send(source, target, send_sem, recv_sem, device):
        pltpu.make_async_remote_copy(
            source, target, send_sem, recv_sem, device_id=device, device_id_type=MESH
        ).start()

    def pack(q, dx, dy):
        for dz in (0, 1):
            target = place.block(dx, dy, dz)
            for k in (0, 1):
                block = elems[places[target * 2 + k]]
                packed[q, dz, k, pl.ds(0, BS), :] = block[:, :LANES]
                packed[q, dz, k, pl.ds(BS, 96), :] = jnp.concatenate(
                    [block[:96, LANES:], block[96:, LANES:]], axis=1
                )

    def hand_on(mine, others, at):
        send(mine, r.at[level, at], es, er, place.above(2))
        send(others, r.at[level, at], es, er, place.above(1))
        send(others, r.at[level, at], es, er, place.above(3))

    def elements(q):
        dx, dy = shift(q)
        pack(q, dx, dy)
        device = place.device(dx, dy, 0)
        send(packed.at[q, 0], r.at[level, spot], ed, ee.at[q], device)
        send(packed.at[q, 1], t.at[spot], ed, eo.at[q], device)
        send(codes, m.at[level, spot], ms, mr, device)

    def own_elements():
        pack(0, 0, 0)
        hand_on(packed.at[0, 0], packed.at[0, 1], spot)
        pltpu.make_async_copy(packed.at[0, 0], r.at[level, spot], ee.at[0]).start()
        pltpu.make_async_copy(packed.at[0, 1], t.at[spot], eo.at[0]).start()
        pltpu.make_async_copy(codes, m.at[level, spot], mr).start()

    def relay(q):
        dx, dy = shift(q)
        at = lax.rem(place.y + 4 - dy, 4) * 4 + lax.rem(place.x + 4 - dx, 4)
        wait_bytes(r.at[level, at], ee.at[q])
        wait_bytes(t.at[at], eo.at[q])
        hand_on(r.at[level, at], t.at[at], at)

    def loop(first, last, step):
        def one(k, _):
            step(k)
            return 0

        lax.fori_loop(first, last, one, 0)

    own_elements()
    loop(1, 5, elements)
    gather.neighbour_z()
    loop(5, 7, elements)
    gather.pass1(0)
    loop(7, 9, elements)
    loop(1, 3, relay)
    gather.pass1(1)
    loop(9, 11, elements)
    loop(3, 5, relay)
    gather.far1(0)
    loop(11, 13, elements)
    loop(5, 6, relay)
    gather.far1(1)
    loop(13, 16, elements)
    loop(6, 7, relay)

    def step2(k):
        gather.pass2(k)
        relay(7 + k)

    loop(0, 8, step2)
    wait_bytes(r.at[level, spot], ee.at[0])
    wait_bytes(t.at[spot], eo.at[0])
    wait_bytes(m.at[level], mr)
    for dz in (1, 2, 3):
        send(m.at[level], m.at[level], mz, mzr, place.above(dz))

    def step3(k):
        gather.far2(k)

        @pl.when(k == 0)
        def _():
            relay(15)

    loop(0, 8, step3)
    gather.finish()
    wait_bytes(r.at[pl.ds(0, 3)], er)
    wait_bytes(m.at[pl.ds(0, 3)], mzr)
    wait_bytes(r.at[pl.ds(0, 3)], es)
    wait_bytes(packed.at[pl.ds(0, 15)], ed)
    wait_bytes(m.at[0, pl.ds(0, 15)], ms)
    wait_bytes(m.at[pl.ds(0, 3)], mz)


def exchange(loads, elems, places, codes):
    any_space = pl.BlockSpec(memory_space=pl.ANY)
    dma = pltpu.SemaphoreType.DMA
    return pl.pallas_call(
        exchange_kernel,
        out_shape=[
            jax.ShapeDtypeStruct((32 * ROWS, 2 * LANES), jnp.bfloat16),
            jax.ShapeDtypeStruct((4, 16, 2, PACKED, LANES), jnp.bfloat16),
            jax.ShapeDtypeStruct((4, 16, 8, LANES), jnp.int32),
            jax.ShapeDtypeStruct((16, 2, PACKED, LANES), jnp.bfloat16),
        ],
        in_specs=[
            any_space,
            pl.BlockSpec(memory_space=pltpu.VMEM),
            pl.BlockSpec(memory_space=pltpu.SMEM),
            any_space,
        ],
        out_specs=[any_space] * 4,
        scratch_shapes=[
            pltpu.VMEM((16, 2, 2, PACKED, LANES), jnp.bfloat16),
            dma,
            dma,
            dma,
            dma((16,)),
            dma((16,)),
            dma,
            dma,
            dma,
            dma,
            dma,
            *gather_scratch(),
        ],
        compiler_params=pltpu.CompilerParams(collective_id=1, has_side_effects=True, vmem_limit_bytes=32 << 20),
        name="exchange",
    )(loads, elems, places, codes)


def share_sum(place, part, came, send_sem, recv_sem):
    lanes = pl.ds(pl.multiple_of(place.core * LANES, LANES), LANES)
    other = pl.ds(pl.multiple_of((1 - place.core) * LANES, LANES), LANES)
    copy = pltpu.make_async_remote_copy(
        part.at[:, other], came, send_sem, recv_sem, device_id=place.device(0, 0, 0, 0, 1), device_id_type=MESH
    )
    copy.start()
    copy.wait()
    return part[:, lanes] + came[...]


def gather_kernel(part, g, came, first, send_sem, recv_sem, own, *sems):
    place = Place()
    gather = Gather(place, g, sems)
    barrier = greet(gather.peers())
    pl.semaphore_wait(barrier, 6)
    first[...] = share_sum(place, part, came, send_sem, recv_sem).astype(jnp.bfloat16)
    mine = pltpu.make_async_copy(first, gather.chunk(0), own)
    mine.start()
    mine.wait()
    gather.start()
    gather.neighbour_z()
    gather.pass1(0)
    gather.pass1(1)
    gather.far1(0)
    gather.far1(1)

    def step2(k, _):
        gather.pass2(k)
        return 0

    lax.fori_loop(0, 8, step2, 0)

    def step3(k, _):
        gather.far2(k)
        return 0

    lax.fori_loop(0, 8, step3, 0)
    gather.finish()


def gather_first(part):
    dma = pltpu.SemaphoreType.DMA
    return pl.pallas_call(
        gather_kernel,
        out_shape=jax.ShapeDtypeStruct((32 * ROWS, 2 * LANES), jnp.bfloat16),
        in_specs=[pl.BlockSpec(memory_space=pltpu.VMEM)],
        out_specs=pl.BlockSpec(memory_space=pl.ANY),
        scratch_shapes=[
            pltpu.VMEM((ROWS, LANES), jnp.float32),
            pltpu.VMEM((ROWS, LANES), jnp.bfloat16),
            dma,
            dma,
            dma,
            *gather_scratch(),
        ],
        compiler_params=pltpu.CompilerParams(collective_id=2, has_side_effects=True, vmem_limit_bytes=16 << 20),
        name="gather_first",
    )(part)


def sum_kernel(part, out, came, send_sem, recv_sem):
    place = Place()
    barrier = greet([place.device(0, 0, 0, 0, 1)])
    pl.semaphore_wait(barrier, 1)
    out[...] = share_sum(place, part, came, send_sem, recv_sem)


def sum_cores(part):
    dma = pltpu.SemaphoreType.DMA
    return pl.pallas_call(
        sum_kernel,
        out_shape=jax.ShapeDtypeStruct((ROWS, LANES), jnp.float32),
        in_specs=[pl.BlockSpec(memory_space=pltpu.VMEM)],
        out_specs=pl.BlockSpec(memory_space=pltpu.VMEM),
        scratch_shapes=[pltpu.VMEM((ROWS, LANES), jnp.float32), dma, dma],
        compiler_params=pltpu.CompilerParams(collective_id=3, has_side_effects=True, vmem_limit_bytes=16 << 20),
        name="sum_cores",
    )(part)


def product_kernel(turn, vrow, vcol, erow, ecol, vals, elems, g, out, panel, vbuf, ebuf, acc, psem, vsem, esem):
    v_count = vals.shape[0] // (2 * CHUNK)
    e_count = elems.shape[0] // CHUNK
    core = turn[0]

    def v_copy(j, slot):
        first = (2 * j + core) * CHUNK
        return pltpu.make_async_copy(vals.at[pl.ds(first, CHUNK)], vbuf.at[slot], vsem.at[slot])

    def e_copy(j, slot):
        return pltpu.make_async_copy(elems.at[pl.ds(j * CHUNK, CHUNK)], ebuf.at[slot], esem.at[slot])

    for q in range(8):
        pltpu.make_async_copy(g.at[pl.ds(q * 16, 16)], panel.at[pl.ds(q * 16, 16)], psem.at[q]).start()
    for j in range(DEPTH):
        v_copy(j, j).start()
        e_copy(j, j).start()
    acc[...] = jnp.zeros_like(acc)
    for q in range(8):
        pltpu.make_async_copy(g.at[pl.ds(q * 16, 16)], panel.at[pl.ds(q * 16, 16)], psem.at[q]).wait()

    def v_step(j, _):
        slot = lax.rem(j, DEPTH)
        v_copy(j, slot).wait()
        for u in range(CHUNK):
            s = (2 * j + core) * CHUNK + u
            acc[vrow[s]] += jnp.dot(vbuf[slot, u], panel[vcol[s]], preferred_element_type=jnp.float32)

        @pl.when(j + DEPTH < v_count)
        def _():
            v_copy(j + DEPTH, slot).start()

        return 0

    lax.fori_loop(0, v_count, v_step, 0)

    def e_step(j, _):
        slot = lax.rem(j, DEPTH)
        e_copy(j, slot).wait()
        for u in range(CHUNK):
            s = j * CHUNK + u
            tail = ebuf[slot, u, pl.ds(BS, 96)]
            right = jnp.concatenate([tail[:, :64], tail[:, 64:]], axis=0)
            block = jnp.concatenate([ebuf[slot, u, pl.ds(0, BS)], right], axis=1)
            acc[erow[s]] += jnp.dot(block, panel[ecol[s]], preferred_element_type=jnp.float32)

        @pl.when(j + DEPTH < e_count)
        def _():
            e_copy(j + DEPTH, slot).start()

        return 0

    lax.fori_loop(0, e_count, e_step, 0)
    out[...] = acc[:4].reshape(out.shape)


def products(turn, vrow, vcol, erow, ecol, vals, elems, g):
    smem = pl.BlockSpec(memory_space=pltpu.SMEM)
    any_space = pl.BlockSpec(memory_space=pl.ANY)
    dma = pltpu.SemaphoreType.DMA
    return pl.pallas_call(
        product_kernel,
        out_shape=jax.ShapeDtypeStruct((ROWS, 2 * LANES), jnp.float32),
        in_specs=[smem] * 5 + [any_space] * 3,
        out_specs=pl.BlockSpec(memory_space=pltpu.VMEM),
        scratch_shapes=[
            pltpu.VMEM((128, BS, 2 * LANES), jnp.bfloat16),
            pltpu.VMEM((DEPTH, CHUNK, BS, BS), jnp.bfloat16),
            pltpu.VMEM((DEPTH, CHUNK, PACKED, LANES), jnp.bfloat16),
            pltpu.VMEM((5, BS, 2 * LANES), jnp.float32),
            dma((8,)),
            dma((DEPTH,)),
            dma((DEPTH,)),
        ],
        compiler_params=pltpu.CompilerParams(vmem_limit_bytes=58 << 20),
        name="products",
    )(turn, vrow, vcol, erow, ecol, vals, elems, g.reshape(128, BS, 2 * LANES))


def body(loads, values, row_ptr, col_idx, elem_vals, elem_owner, elem_row, elem_col):
    owners = elem_owner[:, 0]
    count = owners.shape[0]
    order = jnp.arange(count, dtype=jnp.int32)
    earlier = (owners[:, None] == owners[None, :]) & (order[None, :] < order[:, None])
    rank = jnp.sum(earlier.astype(jnp.int32), axis=1)
    slot = owners * 2 + rank
    taken = slot[None, :] == jnp.arange(LANES, dtype=jnp.int32)[:, None]
    places = jnp.sum(jnp.where(taken, order[None, :], 0), axis=1)
    code = jnp.sum(jnp.where(taken, (elem_row * 128 + elem_col + 1)[None, :], 0), axis=1)
    codes = jnp.broadcast_to(code[None, :], (8, LANES))
    g, r, m, _ = exchange(loads, elem_vals, places, codes)

    blk = lax.axis_index("blk")
    core = lax.rem(lax.axis_index("rep"), 2).astype(jnp.int32)
    mine = lax.dynamic_slice(m.reshape(64, 8, LANES), (0, 0, blk * 2), (64, 1, 2)).reshape(128) - 1
    erow = jnp.where(mine < 0, 4, mine // 128)
    ecol = jnp.where(mine < 0, 0, lax.rem(mine, 128))
    positions = jnp.arange(values.shape[0], dtype=jnp.int32)
    vrow = jnp.sum((positions[:, None] >= row_ptr[0, 1:][None, :]).astype(jnp.int32), axis=1)
    turn = core.reshape(1)
    apply = functools.partial(products, turn, vrow, col_idx, erow, ecol, values, r.reshape(128, PACKED, LANES))
    part = apply(g)
    g2 = gather_first(part)
    return sum_cores(apply(g2))


def solution(mesh):
    placed = (
        P("blk", "rep"),
        P("blk", None, None),
        P("blk", None),
        P("blk"),
        P(("blk", "rep"), None, None),
        P(("blk", "rep"), None),
        P(("blk", "rep")),
        P(("blk", "rep")),
    )
    return jax.shard_map(body, mesh=mesh, in_specs=placed, out_specs=P("blk", "rep"), check_vma=False)
```

```python
import functools

import jax
import jax.numpy as jnp
from jax import lax
from jax.experimental import pallas as pl
from jax.experimental.pallas import tpu as pltpu
from jax.sharding import PartitionSpec as P

MESH = pl.DeviceIdType.MESH
BS = 192
ROWS = 768
LANES = 128
HALF = ROWS // 2
PAIR = 3 * BS
CHUNK = 16
DEPTH = 4


class Place:
    def __init__(self):
        blk = lax.axis_index("blk")
        rep = lax.axis_index("rep")
        self.x = lax.rem(blk, 4)
        self.zl = lax.rem(blk // 4, 2)
        self.y = blk // 8
        self.zh = rep // 2
        self.core = lax.rem(rep, 2)

    def block(self, dx, dy, dz):
        x = lax.rem(self.x + dx, 4)
        y = lax.rem(self.y + dy, 4)
        zl = lax.rem(self.zl + dz, 2)
        return (y * 2 + zl) * 4 + x

    def above(self, dz):
        z = lax.rem(self.zh * 2 + self.zl + dz, 4)
        return ((self.y * 2 + lax.rem(z, 2)) * 4 + self.x, (z // 2) * 2 + self.core)

    def device(self, dx, dy, dz, dzh=0, dcore=0):
        zh = lax.rem(self.zh + dzh, 2)
        core = lax.rem(self.core + dcore, 2)
        return (self.block(dx, dy, dz), zh * 2 + core)


SHIFTS = (
    (0, 0), (2, 2), (1, 1), (3, 3), (1, 3), (3, 1), (2, 1), (2, 3),
    (1, 2), (3, 2), (1, 0), (3, 0), (0, 1), (0, 3), (2, 0), (0, 2),
)


def shift(q):
    dx = dy = 0
    for i, (a, b) in enumerate(SHIFTS):
        dx = jnp.where(q == i, a, dx)
        dy = jnp.where(q == i, b, dy)
    return dx, dy


def wait_bytes(ref, sem):
    pltpu.make_async_copy(ref, ref, sem).wait()


class Gather:
    def __init__(self, place, g, late, sems):
        self.place = place
        self.g = g
        self.late = late
        (self.sends, self.cross_s, self.cross_r, self.sem_z, self.sem1, self.sem1f, self.sem2, self.sem2f, self.sem_l) = sems
        self.lanes = pl.ds(pl.multiple_of(place.core * LANES, LANES), LANES)
        self.other = pl.ds(pl.multiple_of((1 - place.core) * LANES, LANES), LANES)

    def peers(self):
        p = self.place
        return [
            p.device(0, 0, 1),
            p.device(1, 0, 0),
            p.device(3, 0, 0),
            p.device(0, 1, 0),
            p.device(0, 3, 0),
            p.device(0, 0, 0, 0, 1),
        ]

    def rows(self, dz):
        return HALF if dz == 0 else HALF - self.late

    def piece(self, half, p1, p2, dz, start=0, size=None):
        block = self.place.block(p1, p2, dz) if half == 0 else self.place.block(p2, p1, dz)
        first = pl.multiple_of(block * ROWS + (half * HALF + start), 64)
        return self.g.at[pl.ds(first, self.rows(dz) if size is None else size), self.lanes]

    def part(self, half, p1, p2, dz, way):
        size = self.rows(dz) // 2
        return self.piece(half, p1, p2, dz, way * size, size)

    def peer(self, half, stage, step):
        along_x = (half == 0) == (stage == 1)
        return self.place.device(step, 0, 0) if along_x else self.place.device(0, step, 0)

    def send(self, ref, device, sem):
        pltpu.make_async_remote_copy(ref, ref, self.sends, sem, device_id=device, device_id_type=MESH).start()

    def cross(self, ref):
        pltpu.make_async_remote_copy(
            ref, ref, self.cross_s, self.cross_r, device_id=self.place.device(0, 0, 0, 0, 1), device_id_type=MESH
        ).start()

    def chunk(self):
        first = pl.multiple_of(self.place.block(0, 0, 0) * ROWS, ROWS)
        return self.g.at[pl.ds(first, ROWS), self.lanes]

    def start(self):
        for half in (0, 1):
            self.send(
                self.piece(half, 0, 0, 0, 0, HALF - self.late), self.place.device(0, 0, 1), self.sem_z.at[half]
            )
        self.spread1(0)
        for half in (0, 1):
            self.spread2(half, 0, 0, 0)
            self.give_late(half, 0, 0)
        self.cross(self.chunk())

    def spread1(self, dz):
        for half in (0, 1):
            for way in (0, 1):
                self.send(
                    self.piece(half, 0, 0, dz), self.peer(half, 1, 1 if way == 0 else 3), self.sem1.at[half, dz, way]
                )

    def spread2(self, half, q, p1, dz):
        for way in (0, 1):
            self.send(
                self.piece(half, p1, 0, dz), self.peer(half, 2, 1 if way == 0 else 3), self.sem2.at[half, q, dz, way]
            )

    def give_late(self, half, p1, p2):
        if self.late:
            self.send(
                self.piece(half, p1, p2, 0, HALF - self.late, self.late),
                self.place.device(0, 0, 1),
                self.sem_l.at[half, p1, p2],
            )

    def take_late(self, p1, p2):
        if self.late:
            for half in (0, 1):
                got = self.piece(half, p1, p2, 1, HALF - self.late, self.late)
                wait_bytes(got, self.sem_l.at[half, p1, p2])
                self.cross(got)

    def neighbour_z(self):
        for half in (0, 1):
            wait_bytes(self.piece(half, 0, 0, 1), self.sem_z.at[half])
        self.spread1(1)
        for half in (0, 1):
            self.spread2(half, 0, 0, 1)
            self.cross(self.piece(half, 0, 0, 1))

    def pass1(self, dz):
        for half in (0, 1):
            for way in (0, 1):
                p1 = 3 if way == 0 else 1
                got = self.piece(half, p1, 0, dz)
                wait_bytes(got, self.sem1.at[half, dz, way])
                self.send(
                    self.part(half, p1, 0, dz, way),
                    self.peer(half, 1, 1 if way == 0 else 3),
                    self.sem1f.at[half, dz, way],
                )
                self.spread2(half, 2 if p1 == 3 else 1, p1, dz)
                self.cross(got)
                if dz == 0:
                    self.give_late(half, p1, 0)

    def far1(self, dz):
        for half in (0, 1):
            for way in (0, 1):
                wait_bytes(self.part(half, 2, 0, dz, way), self.sem1f.at[half, dz, way])
            self.spread2(half, 3, 2, dz)
            self.cross(self.piece(half, 2, 0, dz))
            if dz == 0:
                self.give_late(half, 2, 0)

    def pass2(self, q, dz):
        p1 = q ^ (q // 2)
        for half in (0, 1):
            for way in (0, 1):
                p2 = 3 if way == 0 else 1
                got = self.piece(half, p1, p2, dz)
                wait_bytes(got, self.sem2.at[half, q, dz, way])
                self.send(
                    self.part(half, p1, p2, dz, way),
                    self.peer(half, 2, 1 if way == 0 else 3),
                    self.sem2f.at[half, q, dz, way],
                )
                self.cross(got)
                if dz == 0:
                    self.give_late(half, p1, p2)

    def far2(self, q, dz):
        p1 = q ^ (q // 2)
        for half in (0, 1):
            for way in (0, 1):
                wait_bytes(self.part(half, p1, 2, dz, way), self.sem2f.at[half, q, dz, way])
            self.cross(self.piece(half, p1, 2, dz))
            if dz == 0:
                self.give_late(half, p1, 2)

    def finish(self):
        wait_bytes(self.g.at[:, self.other], self.cross_r)
        wait_bytes(self.g.at[:, self.lanes], self.cross_s)
        wait_bytes(self.g.at[pl.ds(0, 31 * ROWS), self.lanes], self.sends)


def gather_scratch():
    dma = pltpu.SemaphoreType.DMA
    return [
        dma,
        dma,
        dma,
        dma((2,)),
        dma((2, 2, 2)),
        dma((2, 2, 2)),
        dma((2, 4, 2, 2)),
        dma((2, 4, 2, 2)),
        dma((2, 4, 4)),
    ]


def greet(devices):
    barrier = pltpu.get_barrier_semaphore()
    for device in devices:
        pl.semaphore_signal(barrier, inc=1, device_id=device, device_id_type=MESH)
    return barrier


def exchange_kernel(loads, elems, places, codes, g, r, m, t, held, packed, ed, es, er, ee, eo, ms, mz, mr, mzr, own, hsem, *sems):
    place = Place()
    r = r.reshape(4, 16, PAIR, LANES)
    m = m.reshape(4, 16, 8, LANES)
    gather = Gather(place, g.reshape(32 * ROWS, 2 * LANES), 0, sems)
    spot = place.y * 4 + place.x
    level = place.zh * 2 + place.zl
    barrier = greet(gather.peers() + [place.above(dz) for dz in (1, 2, 3)])

    def greet_step(q, _):
        dx, dy = shift(q)
        pl.semaphore_signal(barrier, inc=1, device_id=place.device(dx, dy, 0), device_id_type=MESH)
        return 0

    lax.fori_loop(1, 16, greet_step, 0)
    mine = pltpu.make_async_copy(loads, gather.chunk(), own)
    mine.start()
    holding = pltpu.make_async_copy(elems, held, hsem)
    holding.start()

    mine.wait()
    pl.semaphore_wait(barrier, 6 + 3 + 15)
    gather.start()

    def send(source, target, send_sem, recv_sem, device):
        pltpu.make_async_remote_copy(
            source, target, send_sem, recv_sem, device_id=device, device_id_type=MESH
        ).start()

    def pack(q, dx, dy):
        for dz in (0, 1):
            target = place.block(dx, dy, dz)
            one = held[places[target * 2]]
            two = held[places[target * 2 + 1]]
            packed[q, dz, pl.ds(0, BS), :] = one[:, :LANES]
            packed[q, dz, pl.ds(BS, BS), :] = two[:, :LANES]
            packed[q, dz, pl.ds(2 * BS, BS), :] = jnp.concatenate([one[:, LANES:], two[:, LANES:]], axis=1)

    def hand_on(mine, others, at):
        send(mine, r.at[level, at], es, er, place.above(2))
        send(others, r.at[level, at], es, er, place.above(1))
        send(others, r.at[level, at], es, er, place.above(3))

    def elements(q):
        dx, dy = shift(q)
        pack(q, dx, dy)
        device = place.device(dx, dy, 0)
        send(packed.at[q, 0], r.at[level, spot], ed, ee.at[q], device)
        send(packed.at[q, 1], t.at[spot], ed, eo.at[q], device)
        send(codes, m.at[level, spot], ms, mr, device)

    def own_elements():
        pack(0, 0, 0)
        hand_on(packed.at[0, 0], packed.at[0, 1], spot)
        pltpu.make_async_copy(packed.at[0, 0], r.at[level, spot], ee.at[0]).start()
        pltpu.make_async_copy(packed.at[0, 1], t.at[spot], eo.at[0]).start()
        pltpu.make_async_copy(codes, m.at[level, spot], mr).start()

    def relay(q):
        dx, dy = shift(q)
        at = lax.rem(place.y + 4 - dy, 4) * 4 + lax.rem(place.x + 4 - dx, 4)
        wait_bytes(r.at[level, at], ee.at[q])
        wait_bytes(t.at[at], eo.at[q])
        hand_on(r.at[level, at], t.at[at], at)

    def loop(first, last, step):
        def one(k, _):
            step(k)
            return 0

        lax.fori_loop(first, last, one, 0)

    holding.wait()
    own_elements()
    loop(1, 5, elements)
    gather.neighbour_z()
    loop(5, 7, elements)
    gather.pass1(0)
    loop(7, 9, elements)
    loop(1, 3, relay)
    gather.pass1(1)
    loop(9, 11, elements)
    loop(3, 5, relay)
    gather.far1(0)
    loop(11, 13, elements)
    loop(5, 6, relay)
    gather.far1(1)
    loop(13, 16, elements)
    loop(6, 7, relay)

    def step2(q):
        gather.pass2(q, 0)
        gather.pass2(q, 1)
        relay(7 + 2 * q)
        relay(8 + 2 * q)

    loop(0, 4, step2)
    wait_bytes(r.at[level, spot], ee.at[0])
    wait_bytes(t.at[spot], eo.at[0])
    wait_bytes(m.at[level], mr)
    for dz in (1, 2, 3):
        send(m.at[level], m.at[level], mz, mzr, place.above(dz))

    relay(15)

    def step3(q):
        gather.far2(q, 0)
        gather.far2(q, 1)

    loop(0, 4, step3)
    gather.finish()
    wait_bytes(r.at[pl.ds(0, 3)], er)
    wait_bytes(m.at[pl.ds(0, 3)], mzr)
    wait_bytes(r.at[pl.ds(0, 3)], es)
    wait_bytes(packed.at[pl.ds(0, 15)], ed)
    wait_bytes(m.at[0, pl.ds(0, 15)], ms)
    wait_bytes(m.at[pl.ds(0, 3)], mz)


def exchange(loads, elems, places, codes):
    hbm = pl.BlockSpec(memory_space=pltpu.HBM)
    vmem = pl.BlockSpec(memory_space=pltpu.VMEM)
    dma = pltpu.SemaphoreType.DMA
    return pl.pallas_call(
        exchange_kernel,
        out_shape=[
            pltpu.VMEM((128, BS, 2 * LANES), jnp.bfloat16),
            pltpu.VMEM((64, PAIR, LANES), jnp.bfloat16),
            pltpu.HBM((64, 8, LANES), jnp.int32),
        ],
        in_specs=[
            hbm,
            hbm,
            pl.BlockSpec(memory_space=pltpu.SMEM),
            hbm,
        ],
        out_specs=[vmem, vmem, hbm],
        scratch_shapes=[
            pltpu.VMEM((16, PAIR, LANES), jnp.bfloat16),
            pltpu.VMEM(elems.shape, jnp.bfloat16),
            pltpu.VMEM((16, 2, PAIR, LANES), jnp.bfloat16),
            dma,
            dma,
            dma,
            dma((16,)),
            dma((16,)),
            dma,
            dma,
            dma,
            dma,
            dma,
            dma,
            *gather_scratch(),
        ],
        compiler_params=pltpu.CompilerParams(collective_id=1, has_side_effects=True, vmem_limit_bytes=30 << 20),
        name="exchange",
    )(loads, elems, places, codes)


def share_sum(place, part, came, send_sem, recv_sem):
    lanes = pl.ds(pl.multiple_of(place.core * LANES, LANES), LANES)
    other = pl.ds(pl.multiple_of((1 - place.core) * LANES, LANES), LANES)
    copy = pltpu.make_async_remote_copy(
        part.at[:, other], came, send_sem, recv_sem, device_id=place.device(0, 0, 0, 0, 1), device_id_type=MESH
    )
    copy.start()
    copy.wait()
    return part[:, lanes] + came[...]


def gather_kernel(part, g, came, send_sem, recv_sem, *sems):
    place = Place()
    gather = Gather(place, g.reshape(32 * ROWS, 2 * LANES), 128, sems)
    barrier = greet(gather.peers())
    pl.semaphore_wait(barrier, 6)
    gather.chunk()[...] = share_sum(place, part, came, send_sem, recv_sem).astype(jnp.bfloat16)
    gather.start()
    gather.pass1(0)
    gather.neighbour_z()
    gather.far1(0)

    def loop(first, last, step):
        def one(q, _):
            step(q)
            return 0

        lax.fori_loop(first, last, one, 0)

    loop(0, 3, lambda q: gather.pass2(q, 0))
    gather.pass1(1)
    loop(3, 4, lambda q: gather.pass2(q, 0))
    gather.far1(1)
    loop(0, 4, lambda q: gather.far2(q, 0))

    def step2(q):
        gather.pass2(q, 1)
        gather.take_late(q, 0)

    loop(0, 4, step2)

    def step3(q):
        gather.far2(q, 1)
        gather.take_late(q, 1)
        gather.take_late(q, 3)

    loop(0, 4, step3)
    loop(0, 4, lambda q: gather.take_late(q, 2))
    gather.finish()


def gather_first(part):
    dma = pltpu.SemaphoreType.DMA
    return pl.pallas_call(
        gather_kernel,
        out_shape=pltpu.VMEM((128, BS, 2 * LANES), jnp.bfloat16),
        in_specs=[pl.BlockSpec(memory_space=pltpu.VMEM)],
        out_specs=pl.BlockSpec(memory_space=pltpu.VMEM),
        scratch_shapes=[
            pltpu.VMEM((ROWS, LANES), jnp.float32),
            dma,
            dma,
            *gather_scratch(),
        ],
        compiler_params=pltpu.CompilerParams(collective_id=2, has_side_effects=True, vmem_limit_bytes=4 << 20),
        name="gather_first",
    )(part)


def sum_kernel(part, out, came, send_sem, recv_sem):
    place = Place()
    barrier = greet([place.device(0, 0, 0, 0, 1)])
    pl.semaphore_wait(barrier, 1)
    out[...] = share_sum(place, part, came, send_sem, recv_sem)


def sum_cores(part):
    dma = pltpu.SemaphoreType.DMA
    return pl.pallas_call(
        sum_kernel,
        out_shape=jax.ShapeDtypeStruct((ROWS, LANES), jnp.float32),
        in_specs=[pl.BlockSpec(memory_space=pltpu.VMEM)],
        out_specs=pl.BlockSpec(memory_space=pltpu.VMEM),
        scratch_shapes=[pltpu.VMEM((ROWS, LANES), jnp.float32), dma, dma],
        compiler_params=pltpu.CompilerParams(collective_id=3, has_side_effects=True, vmem_limit_bytes=4 << 20),
        name="sum_cores",
    )(part)


def product_kernel(row_of, col_idx, m, vals, pairs, panel, out, vbuf, acc, code, sem, vsem):
    fetch = pltpu.make_async_copy(m.at[:, 0, :], code, sem)
    fetch.start()
    core = lax.rem(lax.axis_index("rep"), 2)
    blk = lax.axis_index("blk")
    v_count = vals.shape[0] // (2 * CHUNK)

    def v_copy(j, slot):
        first = (2 * j + core) * CHUNK
        return pltpu.make_async_copy(vals.at[pl.ds(first, CHUNK)], vbuf.at[slot], vsem.at[slot])

    for j in range(DEPTH):
        v_copy(j, j).start()
    acc[...] = jnp.zeros_like(acc)
    none = jnp.zeros((64, 2 * LANES), jnp.bfloat16)
    fetch.wait()

    def e_step(j, _):
        for u in range(2 * CHUNK):
            at = j * CHUNK + u // 2
            held = code[at, blk * 2 + u % 2]
            row = lax.shift_right_logical(held, 7)
            x = panel[held & 127]
            ends = [x[LANES:], none] if u % 2 == 0 else [none, x[LANES:]]
            block = jnp.concatenate([pairs[at, pl.ds(u % 2 * BS, BS)], pairs[at, pl.ds(2 * BS, BS)]], axis=1)
            acc[row] += jnp.dot(
                block, jnp.concatenate([x[:LANES], *ends], axis=0), preferred_element_type=jnp.float32
            )
        return 0

    lax.fori_loop(0, pairs.shape[0] // CHUNK, e_step, 0)

    def v_step(j, _):
        slot = lax.rem(j, DEPTH)
        v_copy(j, slot).wait()
        for u in range(CHUNK):
            s = (2 * j + core) * CHUNK + u
            acc[row_of[s]] += jnp.dot(vbuf[slot, u], panel[col_idx[s]], preferred_element_type=jnp.float32)

        @pl.when(j + DEPTH < v_count)
        def _():
            v_copy(j + DEPTH, slot).start()

        return 0

    lax.fori_loop(0, v_count, v_step, 0)
    out[...] = acc[1:].reshape(out.shape)


def products(row_of, col_idx, m, vals, elems, g):
    smem = pl.BlockSpec(memory_space=pltpu.SMEM)
    vmem = pl.BlockSpec(memory_space=pltpu.VMEM)
    hbm = pl.BlockSpec(memory_space=pltpu.HBM)
    return pl.pallas_call(
        product_kernel,
        out_shape=pltpu.VMEM((ROWS, 2 * LANES), jnp.float32),
        in_specs=[smem, smem, hbm, hbm, vmem, vmem],
        out_specs=vmem,
        scratch_shapes=[
            pltpu.VMEM((DEPTH, CHUNK, BS, BS), jnp.bfloat16),
            pltpu.VMEM((5, BS, 2 * LANES), jnp.float32),
            pltpu.SMEM((64, LANES), jnp.int32),
            pltpu.SemaphoreType.DMA,
            pltpu.SemaphoreType.DMA((DEPTH,)),
        ],
        compiler_params=pltpu.CompilerParams(vmem_limit_bytes=12 << 20),
        name="products",
    )(row_of, col_idx, m, vals, elems, g)


def body(loads, values, row_ptr, col_idx, elem_vals, elem_owner, elem_row, elem_col):
    owners = elem_owner[:, 0]
    count = owners.shape[0]
    order = jnp.arange(count, dtype=jnp.int32)
    earlier = (owners[:, None] == owners[None, :]) & (order[None, :] < order[:, None])
    rank = jnp.sum(earlier.astype(jnp.int32), axis=1)
    slot = owners * 2 + rank
    taken = slot[None, :] == jnp.arange(LANES, dtype=jnp.int32)[:, None]
    places = jnp.sum(jnp.where(taken, order[None, :], 0), axis=1)
    code = jnp.sum(jnp.where(taken, ((elem_row + 1) * 128 + elem_col)[None, :], 0), axis=1)
    codes = jnp.broadcast_to(code[None, :], (8, LANES))
    positions = jnp.arange(values.shape[0], dtype=jnp.int32)
    row = 1 + jnp.sum((positions[:, None] >= row_ptr[0, 1:][None, :]).astype(jnp.int32), axis=1)
    row_of = jnp.where(row > 4, 0, row)
    g, r, m = exchange(loads, elem_vals, places, codes)

    apply = functools.partial(products, row_of, col_idx, m, values, r)
    part = apply(g)
    g2 = gather_first(part)
    return sum_cores(apply(g2))


def solution(mesh):
    placed = (
        P("blk", "rep"),
        P("blk", None, None),
        P("blk", None),
        P("blk"),
        P(("blk", "rep"), None, None),
        P(("blk", "rep"), None),
        P(("blk", "rep")),
        P(("blk", "rep")),
    )
    return jax.shard_map(body, mesh=mesh, in_specs=placed, out_specs=P("blk", "rep"), check_vma=False)
```

```python
import functools

import jax
import jax.numpy as jnp
from jax import lax
from jax.experimental import pallas as pl
from jax.experimental.pallas import tpu as pltpu
from jax.sharding import PartitionSpec as P

MESH = pl.DeviceIdType.MESH
BS = 192
ROWS = 768
LANES = 128
HALF = ROWS // 2
PAIR = 3 * BS
CHUNK = 16
DEPTH = 4


class Place:
    def __init__(self):
        blk = lax.axis_index("blk")
        rep = lax.axis_index("rep")
        self.x = lax.rem(blk, 4)
        self.zl = lax.rem(blk // 4, 2)
        self.y = blk // 8
        self.zh = rep // 2
        self.core = lax.rem(rep, 2)

    def block(self, dx, dy, dz):
        x = lax.rem(self.x + dx, 4)
        y = lax.rem(self.y + dy, 4)
        zl = lax.rem(self.zl + dz, 2)
        return (y * 2 + zl) * 4 + x

    def above(self, dz):
        z = lax.rem(self.zh * 2 + self.zl + dz, 4)
        return ((self.y * 2 + lax.rem(z, 2)) * 4 + self.x, (z // 2) * 2 + self.core)

    def device(self, dx, dy, dz, dzh=0, dcore=0):
        zh = lax.rem(self.zh + dzh, 2)
        core = lax.rem(self.core + dcore, 2)
        return (self.block(dx, dy, dz), zh * 2 + core)


SHIFTS = (
    (0, 0), (2, 2), (1, 1), (3, 3), (1, 3), (3, 1), (2, 1), (2, 3),
    (1, 2), (3, 2), (1, 0), (3, 0), (0, 1), (0, 3), (2, 0), (0, 2),
)


def shift(q):
    dx = dy = 0
    for i, (a, b) in enumerate(SHIFTS):
        dx = jnp.where(q == i, a, dx)
        dy = jnp.where(q == i, b, dy)
    return dx, dy


def wait_bytes(ref, sem):
    pltpu.make_async_copy(ref, ref, sem).wait()


class Gather:
    def __init__(self, place, g, late, sems):
        self.place = place
        self.g = g
        self.late = late
        (self.sends, self.cross_s, self.cross_r, self.sem_z, self.sem1, self.sem1f, self.sem2, self.sem2f, self.sem_l) = sems
        self.lanes = pl.ds(pl.multiple_of(place.core * LANES, LANES), LANES)
        self.other = pl.ds(pl.multiple_of((1 - place.core) * LANES, LANES), LANES)

    def peers(self):
        p = self.place
        return [
            p.device(0, 0, 1),
            p.device(1, 0, 0),
            p.device(3, 0, 0),
            p.device(0, 1, 0),
            p.device(0, 3, 0),
            p.device(0, 0, 0, 0, 1),
        ]

    def rows(self, dz):
        return HALF if dz == 0 else HALF - self.late

    def piece(self, half, p1, p2, dz, start=0, size=None):
        block = self.place.block(p1, p2, dz) if half == 0 else self.place.block(p2, p1, dz)
        first = pl.multiple_of(block * ROWS + (half * HALF + start), 64)
        return self.g.at[pl.ds(first, self.rows(dz) if size is None else size), self.lanes]

    def part(self, half, p1, p2, dz, way):
        size = self.rows(dz) // 2
        return self.piece(half, p1, p2, dz, way * size, size)

    def peer(self, half, stage, step):
        along_x = (half == 0) == (stage == 1)
        return self.place.device(step, 0, 0) if along_x else self.place.device(0, step, 0)

    def send(self, ref, device, sem):
        pltpu.make_async_remote_copy(ref, ref, self.sends, sem, device_id=device, device_id_type=MESH).start()

    def cross(self, ref):
        pltpu.make_async_remote_copy(
            ref, ref, self.cross_s, self.cross_r, device_id=self.place.device(0, 0, 0, 0, 1), device_id_type=MESH
        ).start()

    def chunk(self):
        first = pl.multiple_of(self.place.block(0, 0, 0) * ROWS, ROWS)
        return self.g.at[pl.ds(first, ROWS), self.lanes]

    def start(self):
        for half in (0, 1):
            self.send(
                self.piece(half, 0, 0, 0, 0, HALF - self.late), self.place.device(0, 0, 1), self.sem_z.at[half]
            )
        self.spread1(0)
        for half in (0, 1):
            self.spread2(half, 0, 0, 0)
            self.give_late(half, 0, 0)
        self.cross(self.chunk())

    def spread1(self, dz):
        for half in (0, 1):
            for way in (0, 1):
                self.send(
                    self.piece(half, 0, 0, dz), self.peer(half, 1, 1 if way == 0 else 3), self.sem1.at[half, dz, way]
                )

    def spread2(self, half, q, p1, dz):
        for way in (0, 1):
            self.send(
                self.piece(half, p1, 0, dz), self.peer(half, 2, 1 if way == 0 else 3), self.sem2.at[half, q, dz, way]
            )

    def give_late(self, half, p1, p2):
        if self.late:
            self.send(
                self.piece(half, p1, p2, 0, HALF - self.late, self.late),
                self.place.device(0, 0, 1),
                self.sem_l.at[half, p1, p2],
            )

    def take_late(self, p1, p2):
        if self.late:
            for half in (0, 1):
                got = self.piece(half, p1, p2, 1, HALF - self.late, self.late)
                wait_bytes(got, self.sem_l.at[half, p1, p2])
                self.cross(got)

    def neighbour_z(self):
        for half in (0, 1):
            wait_bytes(self.piece(half, 0, 0, 1), self.sem_z.at[half])
        self.spread1(1)
        for half in (0, 1):
            self.spread2(half, 0, 0, 1)
            self.cross(self.piece(half, 0, 0, 1))

    def pass1(self, dz):
        for half in (0, 1):
            for way in (0, 1):
                p1 = 3 if way == 0 else 1
                got = self.piece(half, p1, 0, dz)
                wait_bytes(got, self.sem1.at[half, dz, way])
                self.send(
                    self.part(half, p1, 0, dz, way),
                    self.peer(half, 1, 1 if way == 0 else 3),
                    self.sem1f.at[half, dz, way],
                )
                self.spread2(half, 2 if p1 == 3 else 1, p1, dz)
                self.cross(got)
                if dz == 0:
                    self.give_late(half, p1, 0)

    def far1(self, dz):
        for half in (0, 1):
            for way in (0, 1):
                wait_bytes(self.part(half, 2, 0, dz, way), self.sem1f.at[half, dz, way])
            self.spread2(half, 3, 2, dz)
            self.cross(self.piece(half, 2, 0, dz))
            if dz == 0:
                self.give_late(half, 2, 0)

    def pass2(self, q, dz):
        p1 = q ^ (q // 2)
        for half in (0, 1):
            for way in (0, 1):
                p2 = 3 if way == 0 else 1
                got = self.piece(half, p1, p2, dz)
                wait_bytes(got, self.sem2.at[half, q, dz, way])
                self.send(
                    self.part(half, p1, p2, dz, way),
                    self.peer(half, 2, 1 if way == 0 else 3),
                    self.sem2f.at[half, q, dz, way],
                )
                self.cross(got)
                if dz == 0:
                    self.give_late(half, p1, p2)

    def far2(self, q, dz):
        p1 = q ^ (q // 2)
        for half in (0, 1):
            for way in (0, 1):
                wait_bytes(self.part(half, p1, 2, dz, way), self.sem2f.at[half, q, dz, way])
            self.cross(self.piece(half, p1, 2, dz))
            if dz == 0:
                self.give_late(half, p1, 2)

    def finish(self):
        wait_bytes(self.g.at[:, self.other], self.cross_r)
        wait_bytes(self.g.at[:, self.lanes], self.cross_s)
        wait_bytes(self.g.at[pl.ds(0, 31 * ROWS), self.lanes], self.sends)


def gather_scratch():
    dma = pltpu.SemaphoreType.DMA
    return [
        dma,
        dma,
        dma,
        dma((2,)),
        dma((2, 2, 2)),
        dma((2, 2, 2)),
        dma((2, 4, 2, 2)),
        dma((2, 4, 2, 2)),
        dma((2, 4, 4)),
    ]


def greet(devices):
    barrier = pltpu.get_barrier_semaphore()
    for device in devices:
        pl.semaphore_signal(barrier, inc=1, device_id=device, device_id_type=MESH)
    return barrier


def exchange_kernel(loads, elems, places, codes, g, r, table, m, t, held, packed, ed, es, er, ee, eo, ms, mz, mr, mzr, own, hsem, *sems):
    place = Place()
    r = r.reshape(4, 16, PAIR, LANES)
    gather = Gather(place, g.reshape(32 * ROWS, 2 * LANES), 0, sems)
    spot = place.y * 4 + place.x
    level = place.zh * 2 + place.zl
    barrier = greet(gather.peers() + [place.above(dz) for dz in (1, 2, 3)])

    def greet_step(q, _):
        dx, dy = shift(q)
        pl.semaphore_signal(barrier, inc=1, device_id=place.device(dx, dy, 0), device_id_type=MESH)
        return 0

    lax.fori_loop(1, 16, greet_step, 0)
    mine = pltpu.make_async_copy(loads, gather.chunk(), own)
    mine.start()
    holding = pltpu.make_async_copy(elems, held, hsem)
    holding.start()

    mine.wait()
    pl.semaphore_wait(barrier, 6 + 3 + 15)

    def send(source, target, send_sem, recv_sem, device):
        pltpu.make_async_remote_copy(
            source, target, send_sem, recv_sem, device_id=device, device_id_type=MESH
        ).start()

    def pack(q, dx, dy):
        for dz in (0, 1):
            target = place.block(dx, dy, dz)
            one = held[places[target * 2]]
            two = held[places[target * 2 + 1]]
            packed[q, dz, pl.ds(0, BS), :] = one[:, :LANES]
            packed[q, dz, pl.ds(BS, BS), :] = two[:, :LANES]
            packed[q, dz, pl.ds(2 * BS, BS), :] = jnp.concatenate([one[:, LANES:], two[:, LANES:]], axis=1)

    def hand_on(mine, others, at):
        send(mine, r.at[level, at], es, er, place.above(2))
        send(others, r.at[level, at], es, er, place.above(1))
        send(others, r.at[level, at], es, er, place.above(3))

    def elements(q):
        dx, dy = shift(q)
        pack(q, dx, dy)
        device = place.device(dx, dy, 0)
        send(packed.at[q, 0], r.at[level, spot], ed, ee.at[q], device)
        send(packed.at[q, 1], t.at[spot], ed, eo.at[q], device)
        send(codes, m.at[level, spot], ms, mr, device)

    def own_elements():
        pack(0, 0, 0)
        hand_on(packed.at[0, 0], packed.at[0, 1], spot)
        pltpu.make_async_copy(packed.at[0, 0], r.at[level, spot], ee.at[0]).start()
        pltpu.make_async_copy(packed.at[0, 1], t.at[spot], eo.at[0]).start()
        pltpu.make_async_copy(codes, m.at[level, spot], mr).start()

    def relay(q):
        dx, dy = shift(q)
        at = lax.rem(place.y + 4 - dy, 4) * 4 + lax.rem(place.x + 4 - dx, 4)
        wait_bytes(r.at[level, at], ee.at[q])
        wait_bytes(t.at[at], eo.at[q])
        hand_on(r.at[level, at], t.at[at], at)

    def loop(first, last, step):
        def one(k, _):
            step(k)
            return 0

        lax.fori_loop(first, last, one, 0)

    holding.wait()
    own_elements()
    loop(1, 16, elements)
    gather.start()
    loop(1, 16, relay)
    gather.pass1(0)
    gather.neighbour_z()
    gather.far1(0)
    loop(0, 3, lambda q: gather.pass2(q, 0))
    gather.pass1(1)
    loop(3, 4, lambda q: gather.pass2(q, 0))
    gather.far1(1)
    loop(0, 4, lambda q: gather.far2(q, 0))
    loop(0, 4, lambda q: gather.pass2(q, 1))
    loop(0, 4, lambda q: gather.far2(q, 1))
    wait_bytes(r.at[level, spot], ee.at[0])
    wait_bytes(t.at[spot], eo.at[0])
    wait_bytes(m.at[level], mr)
    for dz in (1, 2, 3):
        send(m.at[level], m.at[level], mz, mzr, place.above(dz))
    gather.finish()
    wait_bytes(r.at[pl.ds(0, 3)], er)
    wait_bytes(m.at[pl.ds(0, 3)], mzr)
    wait_bytes(r.at[pl.ds(0, 3)], es)
    wait_bytes(packed.at[pl.ds(0, 15)], ed)
    wait_bytes(m.at[0, pl.ds(0, 15)], ms)
    wait_bytes(m.at[pl.ds(0, 3)], mz)
    table[...] = m[:, :, 0, :].reshape(64, LANES)


def exchange(loads, elems, places, codes):
    hbm = pl.BlockSpec(memory_space=pltpu.HBM)
    vmem = pl.BlockSpec(memory_space=pltpu.VMEM)
    dma = pltpu.SemaphoreType.DMA
    return pl.pallas_call(
        exchange_kernel,
        out_shape=[
            pltpu.VMEM((128, BS, 2 * LANES), jnp.bfloat16),
            pltpu.VMEM((64, PAIR, LANES), jnp.bfloat16),
            pltpu.VMEM((64, LANES), jnp.int32),
        ],
        in_specs=[
            hbm,
            hbm,
            pl.BlockSpec(memory_space=pltpu.SMEM),
            hbm,
        ],
        out_specs=[vmem, vmem, vmem],
        scratch_shapes=[
            pltpu.VMEM((4, 16, 8, LANES), jnp.int32),
            pltpu.VMEM((16, PAIR, LANES), jnp.bfloat16),
            pltpu.VMEM(elems.shape, jnp.bfloat16),
            pltpu.VMEM((16, 2, PAIR, LANES), jnp.bfloat16),
            dma,
            dma,
            dma,
            dma((16,)),
            dma((16,)),
            dma,
            dma,
            dma,
            dma,
            dma,
            dma,
            *gather_scratch(),
        ],
        compiler_params=pltpu.CompilerParams(collective_id=1, has_side_effects=True, vmem_limit_bytes=30 << 20),
        name="exchange",
    )(loads, elems, places, codes)


def share_sum(place, part, came, send_sem, recv_sem):
    lanes = pl.ds(pl.multiple_of(place.core * LANES, LANES), LANES)
    other = pl.ds(pl.multiple_of((1 - place.core) * LANES, LANES), LANES)
    copy = pltpu.make_async_remote_copy(
        part.at[:, other], came, send_sem, recv_sem, device_id=place.device(0, 0, 0, 0, 1), device_id_type=MESH
    )
    copy.start()
    copy.wait()
    return part[:, lanes] + came[...]


def gather_kernel(part, g, came, send_sem, recv_sem, *sems):
    place = Place()
    gather = Gather(place, g.reshape(32 * ROWS, 2 * LANES), 128, sems)
    barrier = greet(gather.peers())
    pl.semaphore_wait(barrier, 6)
    gather.chunk()[...] = share_sum(place, part, came, send_sem, recv_sem).astype(jnp.bfloat16)
    gather.start()
    gather.pass1(0)
    gather.neighbour_z()
    gather.far1(0)

    def loop(first, last, step):
        def one(q, _):
            step(q)
            return 0

        lax.fori_loop(first, last, one, 0)

    loop(0, 3, lambda q: gather.pass2(q, 0))
    gather.pass1(1)
    loop(3, 4, lambda q: gather.pass2(q, 0))
    gather.far1(1)
    loop(0, 4, lambda q: gather.far2(q, 0))

    def step2(q):
        gather.pass2(q, 1)
        gather.take_late(q, 0)

    loop(0, 4, step2)

    def step3(q):
        gather.far2(q, 1)
        gather.take_late(q, 1)
        gather.take_late(q, 3)

    loop(0, 4, step3)
    loop(0, 4, lambda q: gather.take_late(q, 2))
    gather.finish()


def gather_first(part):
    dma = pltpu.SemaphoreType.DMA
    return pl.pallas_call(
        gather_kernel,
        out_shape=pltpu.VMEM((128, BS, 2 * LANES), jnp.bfloat16),
        in_specs=[pl.BlockSpec(memory_space=pltpu.VMEM)],
        out_specs=pl.BlockSpec(memory_space=pltpu.VMEM),
        scratch_shapes=[
            pltpu.VMEM((ROWS, LANES), jnp.float32),
            dma,
            dma,
            *gather_scratch(),
        ],
        compiler_params=pltpu.CompilerParams(collective_id=2, has_side_effects=True, vmem_limit_bytes=4 << 20),
        name="gather_first",
    )(part)


def sum_kernel(part, out, came, send_sem, recv_sem):
    place = Place()
    barrier = greet([place.device(0, 0, 0, 0, 1)])
    pl.semaphore_wait(barrier, 1)
    out[...] = share_sum(place, part, came, send_sem, recv_sem)


def sum_cores(part):
    dma = pltpu.SemaphoreType.DMA
    return pl.pallas_call(
        sum_kernel,
        out_shape=jax.ShapeDtypeStruct((ROWS, LANES), jnp.float32),
        in_specs=[pl.BlockSpec(memory_space=pltpu.VMEM)],
        out_specs=pl.BlockSpec(memory_space=pltpu.VMEM),
        scratch_shapes=[pltpu.VMEM((ROWS, LANES), jnp.float32), dma, dma],
        compiler_params=pltpu.CompilerParams(collective_id=3, has_side_effects=True, vmem_limit_bytes=4 << 20),
        name="sum_cores",
    )(part)


def product_kernel(row_of, col_idx, table, vals, pairs, panel, out, vbuf, acc, code, sem, vsem):
    fetch = pltpu.make_async_copy(table, code, sem)
    fetch.start()
    core = lax.rem(lax.axis_index("rep"), 2)
    blk = lax.axis_index("blk")
    v_count = vals.shape[0] // (2 * CHUNK)

    def v_copy(j, slot):
        first = (2 * j + core) * CHUNK
        return pltpu.make_async_copy(vals.at[pl.ds(first, CHUNK)], vbuf.at[slot], vsem.at[slot])

    for j in range(DEPTH):
        v_copy(j, j).start()
    acc[...] = jnp.zeros_like(acc)
    none = jnp.zeros((64, 2 * LANES), jnp.bfloat16)
    fetch.wait()

    def e_step(j, _):
        for u in range(2 * CHUNK):
            at = j * CHUNK + u // 2
            held = code[at, blk * 2 + u % 2]
            row = lax.shift_right_logical(held, 7)
            x = panel[held & 127]
            ends = [x[LANES:], none] if u % 2 == 0 else [none, x[LANES:]]
            block = jnp.concatenate([pairs[at, pl.ds(u % 2 * BS, BS)], pairs[at, pl.ds(2 * BS, BS)]], axis=1)
            acc[row] += jnp.dot(
                block, jnp.concatenate([x[:LANES], *ends], axis=0), preferred_element_type=jnp.float32
            )
        return 0

    lax.fori_loop(0, pairs.shape[0] // CHUNK, e_step, 0)

    def v_step(j, _):
        slot = lax.rem(j, DEPTH)
        v_copy(j, slot).wait()
        for u in range(CHUNK):
            s = (2 * j + core) * CHUNK + u
            acc[row_of[s]] += jnp.dot(vbuf[slot, u], panel[col_idx[s]], preferred_element_type=jnp.float32)

        @pl.when(j + DEPTH < v_count)
        def _():
            v_copy(j + DEPTH, slot).start()

        return 0

    lax.fori_loop(0, v_count, v_step, 0)
    out[...] = acc[1:].reshape(out.shape)


def products(row_of, col_idx, table, vals, elems, g):
    smem = pl.BlockSpec(memory_space=pltpu.SMEM)
    vmem = pl.BlockSpec(memory_space=pltpu.VMEM)
    hbm = pl.BlockSpec(memory_space=pltpu.HBM)
    return pl.pallas_call(
        product_kernel,
        out_shape=pltpu.VMEM((ROWS, 2 * LANES), jnp.float32),
        in_specs=[smem, smem, vmem, hbm, vmem, vmem],
        out_specs=vmem,
        scratch_shapes=[
            pltpu.VMEM((DEPTH, CHUNK, BS, BS), jnp.bfloat16),
            pltpu.VMEM((5, BS, 2 * LANES), jnp.float32),
            pltpu.SMEM((64, LANES), jnp.int32),
            pltpu.SemaphoreType.DMA,
            pltpu.SemaphoreType.DMA((DEPTH,)),
        ],
        compiler_params=pltpu.CompilerParams(vmem_limit_bytes=12 << 20),
        name="products",
    )(row_of, col_idx, table, vals, elems, g)


def body(loads, values, row_ptr, col_idx, elem_vals, elem_owner, elem_row, elem_col):
    owners = elem_owner[:, 0]
    count = owners.shape[0]
    order = jnp.arange(count, dtype=jnp.int32)
    earlier = (owners[:, None] == owners[None, :]) & (order[None, :] < order[:, None])
    rank = jnp.sum(earlier.astype(jnp.int32), axis=1)
    slot = owners * 2 + rank
    taken = slot[None, :] == jnp.arange(LANES, dtype=jnp.int32)[:, None]
    places = jnp.sum(jnp.where(taken, order[None, :], 0), axis=1)
    code = jnp.sum(jnp.where(taken, ((elem_row + 1) * 128 + elem_col)[None, :], 0), axis=1)
    codes = jnp.broadcast_to(code[None, :], (8, LANES))
    positions = jnp.arange(values.shape[0], dtype=jnp.int32)
    row = 1 + jnp.sum((positions[:, None] >= row_ptr[0, 1:][None, :]).astype(jnp.int32), axis=1)
    row_of = jnp.where(row > 4, 0, row)
    g, r, table = exchange(loads, elem_vals, places, codes)

    apply = functools.partial(products, row_of, col_idx, table, values, r)
    part = apply(g)
    g2 = gather_first(part)
    return sum_cores(apply(g2))


def solution(mesh):
    placed = (
        P("blk", "rep"),
        P("blk", None, None),
        P("blk", None),
        P("blk"),
        P(("blk", "rep"), None, None),
        P(("blk", "rep"), None),
        P(("blk", "rep")),
        P(("blk", "rep")),
    )
    return jax.shard_map(body, mesh=mesh, in_specs=placed, out_specs=P("blk", "rep"), check_vma=False)
```

```python
import functools

import jax
import jax.numpy as jnp
from jax import lax
from jax.experimental import pallas as pl
from jax.experimental.pallas import tpu as pltpu
from jax.sharding import PartitionSpec as P

MESH = pl.DeviceIdType.MESH
BS = 192
ROWS = 768
LANES = 128
HALF = ROWS // 2
PAIR = 3 * BS
CHUNK = 16
DEPTH = 4
STORED_ROWS = ((0, 1, (0,)), (1, 2, (0, 1)), (2, 3, (0, 1, 2)), (3, 5, (1, 2, 3)), (5, 7, (2, 3)), (7, 9, (3,)))


class Place:
    def __init__(self):
        blk = lax.axis_index("blk")
        rep = lax.axis_index("rep")
        self.x = lax.rem(blk, 4)
        self.zl = lax.rem(blk // 4, 2)
        self.y = blk // 8
        self.zh = rep // 2
        self.core = lax.rem(rep, 2)

    def block(self, dx, dy, dz):
        x = lax.rem(self.x + dx, 4)
        y = lax.rem(self.y + dy, 4)
        zl = lax.rem(self.zl + dz, 2)
        return (y * 2 + zl) * 4 + x

    def above(self, dz):
        z = lax.rem(self.zh * 2 + self.zl + dz, 4)
        return ((self.y * 2 + lax.rem(z, 2)) * 4 + self.x, (z // 2) * 2 + self.core)

    def device(self, dx, dy, dz, dzh=0, dcore=0):
        zh = lax.rem(self.zh + dzh, 2)
        core = lax.rem(self.core + dcore, 2)
        return (self.block(dx, dy, dz), zh * 2 + core)


SHIFTS = (
    (0, 0), (2, 2), (1, 1), (3, 3), (1, 3), (3, 1), (2, 1), (2, 3),
    (1, 2), (3, 2), (1, 0), (3, 0), (0, 1), (0, 3), (2, 0), (0, 2),
)


def shift(q):
    dx = dy = 0
    for i, (a, b) in enumerate(SHIFTS):
        dx = jnp.where(q == i, a, dx)
        dy = jnp.where(q == i, b, dy)
    return dx, dy


def wait_bytes(ref, sem):
    pltpu.make_async_copy(ref, ref, sem).wait()


class Gather:
    def __init__(self, place, g, late, sems):
        self.place = place
        self.g = g
        self.late = late
        (self.sends, self.cross_s, self.cross_r, self.sem_z, self.sem1, self.sem1f, self.sem2, self.sem2f, self.sem_l) = sems
        self.lanes = pl.ds(pl.multiple_of(place.core * LANES, LANES), LANES)
        self.other = pl.ds(pl.multiple_of((1 - place.core) * LANES, LANES), LANES)

    def peers(self):
        p = self.place
        return [
            p.device(0, 0, 1),
            p.device(1, 0, 0),
            p.device(3, 0, 0),
            p.device(0, 1, 0),
            p.device(0, 3, 0),
            p.device(0, 0, 0, 0, 1),
        ]

    def rows(self, dz):
        return HALF if dz == 0 else HALF - self.late

    def piece(self, half, p1, p2, dz, start=0, size=None):
        block = self.place.block(p1, p2, dz) if half == 0 else self.place.block(p2, p1, dz)
        first = pl.multiple_of(block * ROWS + (half * HALF + start), 64)
        return self.g.at[pl.ds(first, self.rows(dz) if size is None else size), self.lanes]

    def part(self, half, p1, p2, dz, way):
        size = self.rows(dz) // 2
        return self.piece(half, p1, p2, dz, way * size, size)

    def peer(self, half, stage, step):
        along_x = (half == 0) == (stage == 1)
        return self.place.device(step, 0, 0) if along_x else self.place.device(0, step, 0)

    def send(self, ref, device, sem):
        pltpu.make_async_remote_copy(ref, ref, self.sends, sem, device_id=device, device_id_type=MESH).start()

    def cross(self, ref):
        pltpu.make_async_remote_copy(
            ref, ref, self.cross_s, self.cross_r, device_id=self.place.device(0, 0, 0, 0, 1), device_id_type=MESH
        ).start()

    def chunk(self):
        first = pl.multiple_of(self.place.block(0, 0, 0) * ROWS, ROWS)
        return self.g.at[pl.ds(first, ROWS), self.lanes]

    def start(self):
        for half in (0, 1):
            self.send(
                self.piece(half, 0, 0, 0, 0, HALF - self.late), self.place.device(0, 0, 1), self.sem_z.at[half]
            )
        self.spread1(0)
        for half in (0, 1):
            self.spread2(half, 0, 0, 0)
            self.give_late(half, 0, 0)
        self.cross(self.chunk())

    def spread1(self, dz):
        for half in (0, 1):
            for way in (0, 1):
                self.send(
                    self.piece(half, 0, 0, dz), self.peer(half, 1, 1 if way == 0 else 3), self.sem1.at[half, dz, way]
                )

    def spread2(self, half, q, p1, dz):
        for way in (0, 1):
            self.send(
                self.piece(half, p1, 0, dz), self.peer(half, 2, 1 if way == 0 else 3), self.sem2.at[half, q, dz, way]
            )

    def give_late(self, half, p1, p2):
        if self.late:
            self.send(
                self.piece(half, p1, p2, 0, HALF - self.late, self.late),
                self.place.device(0, 0, 1),
                self.sem_l.at[half, p1, p2],
            )

    def take_late(self, p1, p2):
        if self.late:
            for half in (0, 1):
                got = self.piece(half, p1, p2, 1, HALF - self.late, self.late)
                wait_bytes(got, self.sem_l.at[half, p1, p2])
                self.cross(got)

    def neighbour_z(self):
        for half in (0, 1):
            wait_bytes(self.piece(half, 0, 0, 1), self.sem_z.at[half])
        self.spread1(1)
        for half in (0, 1):
            self.spread2(half, 0, 0, 1)
            self.cross(self.piece(half, 0, 0, 1))

    def pass1(self, dz):
        for half in (0, 1):
            for way in (0, 1):
                p1 = 3 if way == 0 else 1
                got = self.piece(half, p1, 0, dz)
                wait_bytes(got, self.sem1.at[half, dz, way])
                self.send(
                    self.part(half, p1, 0, dz, way),
                    self.peer(half, 1, 1 if way == 0 else 3),
                    self.sem1f.at[half, dz, way],
                )
                self.spread2(half, 2 if p1 == 3 else 1, p1, dz)
                self.cross(got)
                if dz == 0:
                    self.give_late(half, p1, 0)

    def far1(self, dz):
        for half in (0, 1):
            for way in (0, 1):
                wait_bytes(self.part(half, 2, 0, dz, way), self.sem1f.at[half, dz, way])
            self.spread2(half, 3, 2, dz)
            self.cross(self.piece(half, 2, 0, dz))
            if dz == 0:
                self.give_late(half, 2, 0)

    def pass2(self, q, dz):
        p1 = q ^ (q // 2)
        for half in (0, 1):
            for way in (0, 1):
                p2 = 3 if way == 0 else 1
                got = self.piece(half, p1, p2, dz)
                wait_bytes(got, self.sem2.at[half, q, dz, way])
                self.send(
                    self.part(half, p1, p2, dz, way),
                    self.peer(half, 2, 1 if way == 0 else 3),
                    self.sem2f.at[half, q, dz, way],
                )
                self.cross(got)
                if dz == 0:
                    self.give_late(half, p1, p2)

    def far2(self, q, dz):
        p1 = q ^ (q // 2)
        for half in (0, 1):
            for way in (0, 1):
                wait_bytes(self.part(half, p1, 2, dz, way), self.sem2f.at[half, q, dz, way])
            self.cross(self.piece(half, p1, 2, dz))
            if dz == 0:
                self.give_late(half, p1, 2)

    def finish(self):
        wait_bytes(self.g.at[:, self.other], self.cross_r)
        wait_bytes(self.g.at[:, self.lanes], self.cross_s)
        wait_bytes(self.g.at[pl.ds(0, 31 * ROWS), self.lanes], self.sends)


def gather_scratch():
    dma = pltpu.SemaphoreType.DMA
    return [
        dma,
        dma,
        dma,
        dma((2,)),
        dma((2, 2, 2)),
        dma((2, 2, 2)),
        dma((2, 4, 2, 2)),
        dma((2, 4, 2, 2)),
        dma((2, 4, 4)),
    ]


def greet(devices):
    barrier = pltpu.get_barrier_semaphore()
    for device in devices:
        pl.semaphore_signal(barrier, inc=1, device_id=device, device_id_type=MESH)
    return barrier


def exchange_kernel(loads, elems, places, codes, row_of, col_idx, vals, g, r, table, part, m, v, t, held, packed, ed, es, er, ee, eo, ms, mz, mr, mzr, own, hsem, vsem, *sems):
    place = Place()
    r = r.reshape(4, 16, PAIR, LANES)
    gather = Gather(place, g.reshape(32 * ROWS, 2 * LANES), 0, sems)
    spot = place.y * 4 + place.x
    level = place.zh * 2 + place.zl
    barrier = greet(gather.peers() + [place.above(dz) for dz in (1, 2, 3)])

    def greet_step(q, _):
        dx, dy = shift(q)
        pl.semaphore_signal(barrier, inc=1, device_id=place.device(dx, dy, 0), device_id_type=MESH)
        return 0

    lax.fori_loop(1, 16, greet_step, 0)
    mine = pltpu.make_async_copy(loads, gather.chunk(), own)
    mine.start()
    holding = pltpu.make_async_copy(elems, held, hsem)
    holding.start()

    def fetch(j, _):
        first = (2 * j + place.core) * CHUNK
        pltpu.make_async_copy(vals.at[pl.ds(first, CHUNK)], v.at[pl.ds(j * CHUNK, CHUNK)], vsem).start()
        return 0

    lax.fori_loop(0, v.shape[0] // CHUNK, fetch, 0)

    mine.wait()
    pl.semaphore_wait(barrier, 6 + 3 + 15)

    def send(source, target, send_sem, recv_sem, device):
        pltpu.make_async_remote_copy(
            source, target, send_sem, recv_sem, device_id=device, device_id_type=MESH
        ).start()

    def pack(q, dx, dy):
        for dz in (0, 1):
            target = place.block(dx, dy, dz)
            one = held[places[target * 2]]
            two = held[places[target * 2 + 1]]
            packed[q, dz, pl.ds(0, BS), :] = one[:, :LANES]
            packed[q, dz, pl.ds(BS, BS), :] = two[:, :LANES]
            packed[q, dz, pl.ds(2 * BS, BS), :] = jnp.concatenate([one[:, LANES:], two[:, LANES:]], axis=1)

    def hand_on(mine, others, at):
        send(mine, r.at[level, at], es, er, place.above(2))
        send(others, r.at[level, at], es, er, place.above(1))
        send(others, r.at[level, at], es, er, place.above(3))

    def elements(q):
        dx, dy = shift(q)
        pack(q, dx, dy)
        device = place.device(dx, dy, 0)
        send(packed.at[q, 0], r.at[level, spot], ed, ee.at[q], device)
        send(packed.at[q, 1], t.at[spot], ed, eo.at[q], device)
        send(codes, m.at[level, spot], ms, mr, device)

    def own_elements():
        pack(0, 0, 0)
        hand_on(packed.at[0, 0], packed.at[0, 1], spot)
        pltpu.make_async_copy(packed.at[0, 0], r.at[level, spot], ee.at[0]).start()
        pltpu.make_async_copy(packed.at[0, 1], t.at[spot], eo.at[0]).start()
        pltpu.make_async_copy(codes, m.at[level, spot], mr).start()

    def relay(q):
        dx, dy = shift(q)
        at = lax.rem(place.y + 4 - dy, 4) * 4 + lax.rem(place.x + 4 - dx, 4)
        wait_bytes(r.at[level, at], ee.at[q])
        wait_bytes(t.at[at], eo.at[q])
        hand_on(r.at[level, at], t.at[at], at)

    def loop(first, last, step):
        def one(k, _):
            step(k)
            return 0

        lax.fori_loop(first, last, one, 0)

    holding.wait()
    own_elements()
    loop(1, 16, elements)
    gather.start()
    loop(1, 16, relay)
    gather.pass1(0)
    gather.neighbour_z()
    gather.far1(0)
    loop(0, 3, lambda q: gather.pass2(q, 0))
    gather.pass1(1)
    loop(3, 4, lambda q: gather.pass2(q, 0))
    gather.far1(1)
    loop(0, 4, lambda q: gather.far2(q, 0))
    loop(0, 4, lambda q: gather.pass2(q, 1))
    loop(0, 4, lambda q: gather.far2(q, 1))
    wait_bytes(r.at[level, spot], ee.at[0])
    wait_bytes(t.at[spot], eo.at[0])
    wait_bytes(m.at[level], mr)
    for dz in (1, 2, 3):
        send(m.at[level], m.at[level], mz, mzr, place.above(dz))
    part[...] = jnp.zeros_like(part)
    wait_bytes(v, vsem)
    gather.finish()
    for first, last, rows in STORED_ROWS:

        def stored(j):
            for u in range(CHUNK):
                s = (2 * j + place.core) * CHUNK + u
                product = jnp.dot(v[j * CHUNK + u], g[col_idx[s]], preferred_element_type=jnp.float32)
                row = row_of[s]
                for i in rows:
                    part[i] += jnp.where(row == i + 1, product, 0.0)

        loop(first, last, stored)
    wait_bytes(r.at[pl.ds(0, 3)], er)
    wait_bytes(m.at[pl.ds(0, 3)], mzr)
    wait_bytes(r.at[pl.ds(0, 3)], es)
    wait_bytes(packed.at[pl.ds(0, 15)], ed)
    wait_bytes(m.at[0, pl.ds(0, 15)], ms)
    wait_bytes(m.at[pl.ds(0, 3)], mz)
    table[...] = m[:, :, 0, :].reshape(64, LANES)


def exchange(loads, elems, places, codes, row_of, col_idx, vals):
    hbm = pl.BlockSpec(memory_space=pltpu.HBM)
    vmem = pl.BlockSpec(memory_space=pltpu.VMEM)
    dma = pltpu.SemaphoreType.DMA
    return pl.pallas_call(
        exchange_kernel,
        out_shape=[
            pltpu.VMEM((128, BS, 2 * LANES), jnp.bfloat16),
            pltpu.VMEM((64, PAIR, LANES), jnp.bfloat16),
            pltpu.VMEM((64, LANES), jnp.int32),
            pltpu.VMEM((4, BS, 2 * LANES), jnp.float32),
        ],
        in_specs=[
            hbm,
            hbm,
            pl.BlockSpec(memory_space=pltpu.SMEM),
            hbm,
            pl.BlockSpec(memory_space=pltpu.SMEM),
            pl.BlockSpec(memory_space=pltpu.SMEM),
            hbm,
        ],
        out_specs=[vmem] * 4,
        scratch_shapes=[
            pltpu.VMEM((4, 16, 8, LANES), jnp.int32),
            pltpu.VMEM((vals.shape[0] // 2, BS, BS), jnp.bfloat16),
            pltpu.VMEM((16, PAIR, LANES), jnp.bfloat16),
            pltpu.VMEM(elems.shape, jnp.bfloat16),
            pltpu.VMEM((16, 2, PAIR, LANES), jnp.bfloat16),
            dma,
            dma,
            dma,
            dma((16,)),
            dma((16,)),
            dma,
            dma,
            dma,
            dma,
            dma,
            dma,
            dma,
            *gather_scratch(),
        ],
        compiler_params=pltpu.CompilerParams(collective_id=1, has_side_effects=True, vmem_limit_bytes=30 << 20),
        name="exchange",
    )(loads, elems, places, codes, row_of, col_idx, vals)


def share_sum(place, part, came, send_sem, recv_sem):
    lanes = pl.ds(pl.multiple_of(place.core * LANES, LANES), LANES)
    other = pl.ds(pl.multiple_of((1 - place.core) * LANES, LANES), LANES)
    copy = pltpu.make_async_remote_copy(
        part.at[:, other], came, send_sem, recv_sem, device_id=place.device(0, 0, 0, 0, 1), device_id_type=MESH
    )
    copy.start()
    copy.wait()
    return part[:, lanes] + came[...]


def gather_kernel(part, g, came, send_sem, recv_sem, *sems):
    place = Place()
    gather = Gather(place, g.reshape(32 * ROWS, 2 * LANES), 128, sems)
    barrier = greet(gather.peers())
    pl.semaphore_wait(barrier, 6)
    gather.chunk()[...] = share_sum(place, part, came, send_sem, recv_sem).astype(jnp.bfloat16)
    gather.start()
    gather.pass1(0)
    gather.neighbour_z()
    gather.far1(0)

    def loop(first, last, step):
        def one(q, _):
            step(q)
            return 0

        lax.fori_loop(first, last, one, 0)

    loop(0, 3, lambda q: gather.pass2(q, 0))
    gather.pass1(1)
    loop(3, 4, lambda q: gather.pass2(q, 0))
    gather.far1(1)
    loop(0, 4, lambda q: gather.far2(q, 0))

    def step2(q):
        gather.pass2(q, 1)
        gather.take_late(q, 0)

    loop(0, 4, step2)

    def step3(q):
        gather.far2(q, 1)
        gather.take_late(q, 1)
        gather.take_late(q, 3)

    loop(0, 4, step3)
    loop(0, 4, lambda q: gather.take_late(q, 2))
    gather.finish()


def gather_first(part):
    dma = pltpu.SemaphoreType.DMA
    return pl.pallas_call(
        gather_kernel,
        out_shape=pltpu.VMEM((128, BS, 2 * LANES), jnp.bfloat16),
        in_specs=[pl.BlockSpec(memory_space=pltpu.VMEM)],
        out_specs=pl.BlockSpec(memory_space=pltpu.VMEM),
        scratch_shapes=[
            pltpu.VMEM((ROWS, LANES), jnp.float32),
            dma,
            dma,
            *gather_scratch(),
        ],
        compiler_params=pltpu.CompilerParams(collective_id=2, has_side_effects=True, vmem_limit_bytes=4 << 20),
        name="gather_first",
    )(part)


def sum_kernel(part, out, came, send_sem, recv_sem):
    place = Place()
    barrier = greet([place.device(0, 0, 0, 0, 1)])
    pl.semaphore_wait(barrier, 1)
    out[...] = share_sum(place, part, came, send_sem, recv_sem)


def sum_cores(part):
    dma = pltpu.SemaphoreType.DMA
    return pl.pallas_call(
        sum_kernel,
        out_shape=jax.ShapeDtypeStruct((ROWS, LANES), jnp.float32),
        in_specs=[pl.BlockSpec(memory_space=pltpu.VMEM)],
        out_specs=pl.BlockSpec(memory_space=pltpu.VMEM),
        scratch_shapes=[pltpu.VMEM((ROWS, LANES), jnp.float32), dma, dma],
        compiler_params=pltpu.CompilerParams(collective_id=3, has_side_effects=True, vmem_limit_bytes=4 << 20),
        name="sum_cores",
    )(part)


def add_pairs(code, blk, pairs, panel, acc):
    none = jnp.zeros((64, 2 * LANES), jnp.bfloat16)

    def step(j, _):
        for u in range(2 * CHUNK):
            at = j * CHUNK + u // 2
            held = code[at, blk * 2 + u % 2]
            row = lax.shift_right_logical(held, 7)
            x = panel[held & 127]
            ends = [x[LANES:], none] if u % 2 == 0 else [none, x[LANES:]]
            block = jnp.concatenate([pairs[at, pl.ds(u % 2 * BS, BS)], pairs[at, pl.ds(2 * BS, BS)]], axis=1)
            acc[row] += jnp.dot(
                block, jnp.concatenate([x[:LANES], *ends], axis=0), preferred_element_type=jnp.float32
            )
        return 0

    lax.fori_loop(0, pairs.shape[0] // CHUNK, step, 0)


def pair_kernel(start, table, pairs, panel, out, acc, code, sem):
    fetch = pltpu.make_async_copy(table, code, sem)
    fetch.start()
    acc[0] = jnp.zeros_like(acc[0])
    acc[1:] = start[...]
    fetch.wait()
    add_pairs(code, lax.axis_index("blk"), pairs, panel, acc)
    out[...] = acc[1:].reshape(out.shape)


def product_kernel(row_of, col_idx, table, vals, pairs, panel, out, vbuf, acc, code, sem, vsem):
    fetch = pltpu.make_async_copy(table, code, sem)
    fetch.start()
    core = lax.rem(lax.axis_index("rep"), 2)
    v_count = vals.shape[0] // (2 * CHUNK)

    def v_copy(j, slot):
        first = (2 * j + core) * CHUNK
        return pltpu.make_async_copy(vals.at[pl.ds(first, CHUNK)], vbuf.at[slot], vsem.at[slot])

    for j in range(DEPTH):
        v_copy(j, j).start()
    acc[...] = jnp.zeros_like(acc)
    fetch.wait()
    add_pairs(code, lax.axis_index("blk"), pairs, panel, acc)

    def v_step(j, _):
        slot = lax.rem(j, DEPTH)
        v_copy(j, slot).wait()
        for u in range(CHUNK):
            s = (2 * j + core) * CHUNK + u
            acc[row_of[s]] += jnp.dot(vbuf[slot, u], panel[col_idx[s]], preferred_element_type=jnp.float32)

        @pl.when(j + DEPTH < v_count)
        def _():
            v_copy(j + DEPTH, slot).start()

        return 0

    lax.fori_loop(0, v_count, v_step, 0)
    out[...] = acc[1:].reshape(out.shape)


def products(row_of, col_idx, table, vals, pairs, g, start=None):
    smem = pl.BlockSpec(memory_space=pltpu.SMEM)
    vmem = pl.BlockSpec(memory_space=pltpu.VMEM)
    hbm = pl.BlockSpec(memory_space=pltpu.HBM)
    work = [
        pltpu.VMEM((5, BS, 2 * LANES), jnp.float32),
        pltpu.SMEM((64, LANES), jnp.int32),
        pltpu.SemaphoreType.DMA,
    ]
    out = pltpu.VMEM((ROWS, 2 * LANES), jnp.float32)
    if start is not None:
        return pl.pallas_call(
            pair_kernel,
            out_shape=out,
            in_specs=[vmem] * 4,
            out_specs=vmem,
            scratch_shapes=work,
            compiler_params=pltpu.CompilerParams(vmem_limit_bytes=4 << 20),
            name="pairs",
        )(start, table, pairs, g)
    return pl.pallas_call(
        product_kernel,
        out_shape=out,
        in_specs=[smem, smem, vmem, hbm, vmem, vmem],
        out_specs=vmem,
        scratch_shapes=[
            pltpu.VMEM((DEPTH, CHUNK, BS, BS), jnp.bfloat16),
            *work,
            pltpu.SemaphoreType.DMA((DEPTH,)),
        ],
        compiler_params=pltpu.CompilerParams(vmem_limit_bytes=12 << 20),
        name="products",
    )(row_of, col_idx, table, vals, pairs, g)


def body(loads, values, row_ptr, col_idx, elem_vals, elem_owner, elem_row, elem_col):
    owners = elem_owner[:, 0]
    count = owners.shape[0]
    order = jnp.arange(count, dtype=jnp.int32)
    earlier = (owners[:, None] == owners[None, :]) & (order[None, :] < order[:, None])
    rank = jnp.sum(earlier.astype(jnp.int32), axis=1)
    slot = owners * 2 + rank
    taken = slot[None, :] == jnp.arange(LANES, dtype=jnp.int32)[:, None]
    places = jnp.sum(jnp.where(taken, order[None, :], 0), axis=1)
    code = jnp.sum(jnp.where(taken, ((elem_row + 1) * 128 + elem_col)[None, :], 0), axis=1)
    codes = jnp.broadcast_to(code[None, :], (8, LANES))
    positions = jnp.arange(values.shape[0], dtype=jnp.int32)
    row = 1 + jnp.sum((positions[:, None] >= row_ptr[0, 1:][None, :]).astype(jnp.int32), axis=1)
    row_of = jnp.where(row > 4, 0, row)
    g, r, table, part = exchange(loads, elem_vals, places, codes, row_of, col_idx, values)

    apply = functools.partial(products, row_of, col_idx, table, values, r)
    part = apply(g, start=part)
    g2 = gather_first(part)
    return sum_cores(apply(g2))


def solution(mesh):
    placed = (
        P("blk", "rep"),
        P("blk", None, None),
        P("blk", None),
        P("blk"),
        P(("blk", "rep"), None, None),
        P(("blk", "rep"), None),
        P(("blk", "rep")),
        P(("blk", "rep")),
    )
    return jax.shard_map(body, mesh=mesh, in_specs=placed, out_specs=P("blk", "rep"), check_vma=False)
```

```python
import functools

import jax
import jax.numpy as jnp
from jax import lax
from jax.experimental import pallas as pl
from jax.experimental.pallas import tpu as pltpu
from jax.sharding import PartitionSpec as P

MESH = pl.DeviceIdType.MESH
BS = 192
ROWS = 768
LANES = 128
HALF = ROWS // 2
PAIR = 3 * BS
CHUNK = 16
DEPTH = 4
STORED_ROWS = ((0, 1, (0,)), (1, 2, (0, 1)), (2, 3, (0, 1, 2)), (3, 5, (1, 2, 3)), (5, 7, (2, 3)), (7, 9, (3,)))


class Place:
    def __init__(self):
        blk = lax.axis_index("blk")
        rep = lax.axis_index("rep")
        self.x = lax.rem(blk, 4)
        self.zl = lax.rem(blk // 4, 2)
        self.y = blk // 8
        self.zh = rep // 2
        self.core = lax.rem(rep, 2)

    def block(self, dx, dy, dz):
        x = lax.rem(self.x + dx, 4)
        y = lax.rem(self.y + dy, 4)
        zl = lax.rem(self.zl + dz, 2)
        return (y * 2 + zl) * 4 + x

    def above(self, dz):
        z = lax.rem(self.zh * 2 + self.zl + dz, 4)
        return ((self.y * 2 + lax.rem(z, 2)) * 4 + self.x, (z // 2) * 2 + self.core)

    def device(self, dx, dy, dz, dzh=0, dcore=0):
        zh = lax.rem(self.zh + dzh, 2)
        core = lax.rem(self.core + dcore, 2)
        return (self.block(dx, dy, dz), zh * 2 + core)


SHIFTS = (
    (0, 0), (2, 2), (1, 1), (3, 3), (1, 3), (3, 1), (2, 1), (2, 3),
    (1, 2), (3, 2), (1, 0), (3, 0), (0, 1), (0, 3), (2, 0), (0, 2),
)


def shift(q):
    dx = dy = 0
    for i, (a, b) in enumerate(SHIFTS):
        dx = jnp.where(q == i, a, dx)
        dy = jnp.where(q == i, b, dy)
    return dx, dy


def wait_bytes(ref, sem):
    pltpu.make_async_copy(ref, ref, sem).wait()


class Gather:
    def __init__(self, place, g, late, sems):
        self.place = place
        self.g = g
        self.late = late
        (self.sends, self.cross_s, self.cross_r, self.sem_z, self.sem1, self.sem1f, self.sem2, self.sem2f, self.sem_l) = sems
        self.lanes = pl.ds(pl.multiple_of(place.core * LANES, LANES), LANES)
        self.other = pl.ds(pl.multiple_of((1 - place.core) * LANES, LANES), LANES)

    def peers(self):
        p = self.place
        return [
            p.device(0, 0, 1),
            p.device(1, 0, 0),
            p.device(3, 0, 0),
            p.device(0, 1, 0),
            p.device(0, 3, 0),
            p.device(0, 0, 0, 0, 1),
        ]

    def rows(self, dz):
        return HALF if dz == 0 else HALF - self.late

    def piece(self, half, p1, p2, dz, start=0, size=None):
        block = self.place.block(p1, p2, dz) if half == 0 else self.place.block(p2, p1, dz)
        first = pl.multiple_of(block * ROWS + (half * HALF + start), 64)
        return self.g.at[pl.ds(first, self.rows(dz) if size is None else size), self.lanes]

    def part(self, half, p1, p2, dz, way):
        size = self.rows(dz) // 2
        return self.piece(half, p1, p2, dz, way * size, size)

    def peer(self, half, stage, step):
        along_x = (half == 0) == (stage == 1)
        return self.place.device(step, 0, 0) if along_x else self.place.device(0, step, 0)

    def send(self, ref, device, sem):
        pltpu.make_async_remote_copy(ref, ref, self.sends, sem, device_id=device, device_id_type=MESH).start()

    def cross(self, ref):
        pltpu.make_async_remote_copy(
            ref, ref, self.cross_s, self.cross_r, device_id=self.place.device(0, 0, 0, 0, 1), device_id_type=MESH
        ).start()

    def chunk(self):
        first = pl.multiple_of(self.place.block(0, 0, 0) * ROWS, ROWS)
        return self.g.at[pl.ds(first, ROWS), self.lanes]

    def start(self):
        for half in (0, 1):
            self.send(
                self.piece(half, 0, 0, 0, 0, HALF - self.late), self.place.device(0, 0, 1), self.sem_z.at[half]
            )
        self.spread1(0)
        for half in (0, 1):
            self.spread2(half, 0, 0, 0)
            self.give_late(half, 0, 0)
        self.cross(self.chunk())

    def spread1(self, dz):
        for half in (0, 1):
            for way in (0, 1):
                self.send(
                    self.piece(half, 0, 0, dz), self.peer(half, 1, 1 if way == 0 else 3), self.sem1.at[half, dz, way]
                )

    def spread2(self, half, q, p1, dz):
        for way in (0, 1):
            self.send(
                self.piece(half, p1, 0, dz), self.peer(half, 2, 1 if way == 0 else 3), self.sem2.at[half, q, dz, way]
            )

    def give_late(self, half, p1, p2):
        if self.late:
            self.send(
                self.piece(half, p1, p2, 0, HALF - self.late, self.late),
                self.place.device(0, 0, 1),
                self.sem_l.at[half, p1, p2],
            )

    def take_late(self, p1, p2):
        if self.late:
            for half in (0, 1):
                got = self.piece(half, p1, p2, 1, HALF - self.late, self.late)
                wait_bytes(got, self.sem_l.at[half, p1, p2])
                self.cross(got)

    def neighbour_z(self):
        for half in (0, 1):
            wait_bytes(self.piece(half, 0, 0, 1), self.sem_z.at[half])
        self.spread1(1)
        for half in (0, 1):
            self.spread2(half, 0, 0, 1)
            self.cross(self.piece(half, 0, 0, 1))

    def pass1(self, dz):
        for half in (0, 1):
            for way in (0, 1):
                p1 = 3 if way == 0 else 1
                got = self.piece(half, p1, 0, dz)
                wait_bytes(got, self.sem1.at[half, dz, way])
                self.send(
                    self.part(half, p1, 0, dz, way),
                    self.peer(half, 1, 1 if way == 0 else 3),
                    self.sem1f.at[half, dz, way],
                )
                self.spread2(half, 2 if p1 == 3 else 1, p1, dz)
                self.cross(got)
                if dz == 0:
                    self.give_late(half, p1, 0)

    def far1(self, dz):
        for half in (0, 1):
            for way in (0, 1):
                wait_bytes(self.part(half, 2, 0, dz, way), self.sem1f.at[half, dz, way])
            self.spread2(half, 3, 2, dz)
            self.cross(self.piece(half, 2, 0, dz))
            if dz == 0:
                self.give_late(half, 2, 0)

    def pass2(self, q, dz):
        p1 = q ^ (q // 2)
        for half in (0, 1):
            for way in (0, 1):
                p2 = 3 if way == 0 else 1
                got = self.piece(half, p1, p2, dz)
                wait_bytes(got, self.sem2.at[half, q, dz, way])
                self.send(
                    self.part(half, p1, p2, dz, way),
                    self.peer(half, 2, 1 if way == 0 else 3),
                    self.sem2f.at[half, q, dz, way],
                )
                self.cross(got)
                if dz == 0:
                    self.give_late(half, p1, p2)

    def far2(self, q, dz):
        p1 = q ^ (q // 2)
        for half in (0, 1):
            for way in (0, 1):
                wait_bytes(self.part(half, p1, 2, dz, way), self.sem2f.at[half, q, dz, way])
            self.cross(self.piece(half, p1, 2, dz))
            if dz == 0:
                self.give_late(half, p1, 2)

    def finish(self):
        wait_bytes(self.g.at[:, self.other], self.cross_r)
        wait_bytes(self.g.at[:, self.lanes], self.cross_s)
        wait_bytes(self.g.at[pl.ds(0, 31 * ROWS), self.lanes], self.sends)


def gather_scratch():
    dma = pltpu.SemaphoreType.DMA
    return [
        dma,
        dma,
        dma,
        dma((2,)),
        dma((2, 2, 2)),
        dma((2, 2, 2)),
        dma((2, 4, 2, 2)),
        dma((2, 4, 2, 2)),
        dma((2, 4, 4)),
    ]


def greet(devices):
    barrier = pltpu.get_barrier_semaphore()
    for device in devices:
        pl.semaphore_signal(barrier, inc=1, device_id=device, device_id_type=MESH)
    return barrier


def exchange_kernel(loads, elems, places, codes, row_of, col_idx, vals, g, r, table, part, m, near, v, t, held, packed, ed, es, er, ee, eo, ms, mz, mr, mzr, own, hsem, vsem, nsem, *sems):
    place = Place()
    r = r.reshape(4, 16, PAIR, LANES)
    gather = Gather(place, g.reshape(32 * ROWS, 2 * LANES), 0, sems)
    spot = place.y * 4 + place.x
    me = place.block(0, 0, 0)
    level = place.zh * 2 + place.zl
    barrier = greet(gather.peers() + [place.above(dz) for dz in (1, 2, 3)])

    def greet_step(q, _):
        dx, dy = shift(q)
        pl.semaphore_signal(barrier, inc=1, device_id=place.device(dx, dy, 0), device_id_type=MESH)
        return 0

    lax.fori_loop(1, 16, greet_step, 0)
    mine = pltpu.make_async_copy(loads, gather.chunk(), own)
    mine.start()
    holding = pltpu.make_async_copy(elems, held, hsem)
    holding.start()

    def fetch(j, _):
        first = (2 * j + place.core) * CHUNK
        pltpu.make_async_copy(vals.at[pl.ds(first, CHUNK)], v.at[pl.ds(j * CHUNK, CHUNK)], vsem).start()
        return 0

    lax.fori_loop(0, v.shape[0] // CHUNK, fetch, 0)

    mine.wait()
    pl.semaphore_wait(barrier, 6 + 3 + 15)

    def send(source, target, send_sem, recv_sem, device):
        pltpu.make_async_remote_copy(
            source, target, send_sem, recv_sem, device_id=device, device_id_type=MESH
        ).start()

    def pack(q, dx, dy):
        for dz in (0, 1):
            target = place.block(dx, dy, dz)
            one = held[places[target * 2]]
            two = held[places[target * 2 + 1]]
            packed[q, dz, pl.ds(0, BS), :] = one[:, :LANES]
            packed[q, dz, pl.ds(BS, BS), :] = two[:, :LANES]
            packed[q, dz, pl.ds(2 * BS, BS), :] = jnp.concatenate([one[:, LANES:], two[:, LANES:]], axis=1)

    def hand_on(mine, others, at):
        send(mine, r.at[level, at], es, er, place.above(2))
        send(others, r.at[level, at], es, er, place.above(1))
        send(others, r.at[level, at], es, er, place.above(3))

    def elements(q):
        dx, dy = shift(q)
        pack(q, dx, dy)
        device = place.device(dx, dy, 0)
        send(packed.at[q, 0], r.at[level, spot], ed, ee.at[q], device)
        send(packed.at[q, 1], t.at[spot], ed, eo.at[q], device)
        send(codes, m.at[level, spot], ms, mr, device)

    def own_elements():
        pack(0, 0, 0)
        hand_on(packed.at[0, 0], packed.at[0, 1], spot)
        pltpu.make_async_copy(packed.at[0, 0], r.at[level, spot], ee.at[0]).start()
        pltpu.make_async_copy(packed.at[0, 1], t.at[spot], eo.at[0]).start()
        pltpu.make_async_copy(codes, m.at[level, spot], mr).start()

    def relay(q):
        dx, dy = shift(q)
        at = lax.rem(place.y + 4 - dy, 4) * 4 + lax.rem(place.x + 4 - dx, 4)
        wait_bytes(r.at[level, at], ee.at[q])
        wait_bytes(t.at[at], eo.at[q])
        hand_on(r.at[level, at], t.at[at], at)

    def loop(first, last, step):
        def one(k, _):
            step(k)
            return 0

        lax.fori_loop(first, last, one, 0)

    holding.wait()
    own_elements()
    loop(1, 16, elements)
    gather.start()
    loop(1, 16, relay)
    gather.pass1(0)
    gather.neighbour_z()
    gather.far1(0)
    loop(0, 3, lambda q: gather.pass2(q, 0))
    gather.pass1(1)
    loop(3, 4, lambda q: gather.pass2(q, 0))
    gather.far1(1)
    loop(0, 4, lambda q: gather.far2(q, 0))
    loop(0, 4, lambda q: gather.pass2(q, 1))
    loop(0, 4, lambda q: gather.far2(q, 1))
    wait_bytes(r.at[level, spot], ee.at[0])
    wait_bytes(t.at[spot], eo.at[0])
    wait_bytes(m.at[level], mr)
    for dz in (1, 2, 3):
        send(m.at[level], m.at[level], mz, mzr, place.above(dz))
    part[...] = jnp.zeros_like(part)
    wait_bytes(v, vsem)
    gather.finish()
    for first, last, rows in STORED_ROWS:

        def stored(j):
            for u in range(CHUNK):
                s = (2 * j + place.core) * CHUNK + u
                product = jnp.dot(v[j * CHUNK + u], g[col_idx[s]], preferred_element_type=jnp.float32)
                row = row_of[s]
                for i in rows:
                    part[i] += jnp.where(row == i + 1, product, 0.0)

        loop(first, last, stored)
    here = pl.ds(pl.multiple_of(level * 16, 16), 16)
    table[here, :] = m[level, :, 0, :]
    pltpu.make_async_copy(table.at[here], near, nsem).start()
    wait_bytes(near, nsem)

    def arrived(j):
        for u in range(CHUNK):
            at = j * (CHUNK // 2) + u // 2
            row, product = pair_product(near, at, me, u % 2, r.at[level, at], g)
            for i in range(4):
                part[i] += jnp.where(row == i + 1, product, 0.0)

    loop(0, 2, arrived)
    wait_bytes(r.at[pl.ds(0, 3)], er)
    wait_bytes(m.at[pl.ds(0, 3)], mzr)
    wait_bytes(r.at[pl.ds(0, 3)], es)
    wait_bytes(packed.at[pl.ds(0, 15)], ed)
    wait_bytes(m.at[0, pl.ds(0, 15)], ms)
    wait_bytes(m.at[pl.ds(0, 3)], mz)
    table[...] = m[:, :, 0, :].reshape(64, LANES)


def exchange(loads, elems, places, codes, row_of, col_idx, vals):
    hbm = pl.BlockSpec(memory_space=pltpu.HBM)
    vmem = pl.BlockSpec(memory_space=pltpu.VMEM)
    dma = pltpu.SemaphoreType.DMA
    return pl.pallas_call(
        exchange_kernel,
        out_shape=[
            pltpu.VMEM((128, BS, 2 * LANES), jnp.bfloat16),
            pltpu.VMEM((64, PAIR, LANES), jnp.bfloat16),
            pltpu.VMEM((64, LANES), jnp.int32),
            pltpu.VMEM((4, BS, 2 * LANES), jnp.float32),
        ],
        in_specs=[
            hbm,
            hbm,
            pl.BlockSpec(memory_space=pltpu.SMEM),
            hbm,
            pl.BlockSpec(memory_space=pltpu.SMEM),
            pl.BlockSpec(memory_space=pltpu.SMEM),
            hbm,
        ],
        out_specs=[vmem] * 4,
        scratch_shapes=[
            pltpu.VMEM((4, 16, 8, LANES), jnp.int32),
            pltpu.SMEM((16, LANES), jnp.int32),
            pltpu.VMEM((vals.shape[0] // 2, BS, BS), jnp.bfloat16),
            pltpu.VMEM((16, PAIR, LANES), jnp.bfloat16),
            pltpu.VMEM(elems.shape, jnp.bfloat16),
            pltpu.VMEM((16, 2, PAIR, LANES), jnp.bfloat16),
            dma,
            dma,
            dma,
            dma((16,)),
            dma((16,)),
            dma,
            dma,
            dma,
            dma,
            dma,
            dma,
            dma,
            dma,
            *gather_scratch(),
        ],
        compiler_params=pltpu.CompilerParams(collective_id=1, has_side_effects=True, vmem_limit_bytes=30 << 20),
        name="exchange",
    )(loads, elems, places, codes, row_of, col_idx, vals)


def share_sum(place, part, came, send_sem, recv_sem):
    lanes = pl.ds(pl.multiple_of(place.core * LANES, LANES), LANES)
    other = pl.ds(pl.multiple_of((1 - place.core) * LANES, LANES), LANES)
    copy = pltpu.make_async_remote_copy(
        part.at[:, other], came, send_sem, recv_sem, device_id=place.device(0, 0, 0, 0, 1), device_id_type=MESH
    )
    copy.start()
    copy.wait()
    return part[:, lanes] + came[...]


def gather_kernel(part, g, came, send_sem, recv_sem, *sems):
    place = Place()
    gather = Gather(place, g.reshape(32 * ROWS, 2 * LANES), 128, sems)
    barrier = greet(gather.peers())
    pl.semaphore_wait(barrier, 6)
    gather.chunk()[...] = share_sum(place, part, came, send_sem, recv_sem).astype(jnp.bfloat16)
    gather.start()
    gather.pass1(0)
    gather.neighbour_z()
    gather.far1(0)

    def loop(first, last, step):
        def one(q, _):
            step(q)
            return 0

        lax.fori_loop(first, last, one, 0)

    loop(0, 3, lambda q: gather.pass2(q, 0))
    gather.pass1(1)
    loop(3, 4, lambda q: gather.pass2(q, 0))
    gather.far1(1)
    loop(0, 4, lambda q: gather.far2(q, 0))

    def step2(q):
        gather.pass2(q, 1)
        gather.take_late(q, 0)

    loop(0, 4, step2)

    def step3(q):
        gather.far2(q, 1)
        gather.take_late(q, 1)
        gather.take_late(q, 3)

    loop(0, 4, step3)
    loop(0, 4, lambda q: gather.take_late(q, 2))
    gather.finish()


def gather_first(part):
    dma = pltpu.SemaphoreType.DMA
    return pl.pallas_call(
        gather_kernel,
        out_shape=pltpu.VMEM((128, BS, 2 * LANES), jnp.bfloat16),
        in_specs=[pl.BlockSpec(memory_space=pltpu.VMEM)],
        out_specs=pl.BlockSpec(memory_space=pltpu.VMEM),
        scratch_shapes=[
            pltpu.VMEM((ROWS, LANES), jnp.float32),
            dma,
            dma,
            *gather_scratch(),
        ],
        compiler_params=pltpu.CompilerParams(collective_id=2, has_side_effects=True, vmem_limit_bytes=4 << 20),
        name="gather_first",
    )(part)


def sum_kernel(part, out, came, send_sem, recv_sem):
    place = Place()
    barrier = greet([place.device(0, 0, 0, 0, 1)])
    pl.semaphore_wait(barrier, 1)
    out[...] = share_sum(place, part, came, send_sem, recv_sem)


def sum_cores(part):
    dma = pltpu.SemaphoreType.DMA
    return pl.pallas_call(
        sum_kernel,
        out_shape=jax.ShapeDtypeStruct((ROWS, LANES), jnp.float32),
        in_specs=[pl.BlockSpec(memory_space=pltpu.VMEM)],
        out_specs=pl.BlockSpec(memory_space=pltpu.VMEM),
        scratch_shapes=[pltpu.VMEM((ROWS, LANES), jnp.float32), dma, dma],
        compiler_params=pltpu.CompilerParams(collective_id=3, has_side_effects=True, vmem_limit_bytes=4 << 20),
        name="sum_cores",
    )(part)


def pair_product(code, at, blk, k, pair, panel):
    held = code[at, blk * 2 + k]
    none = jnp.zeros((64, 2 * LANES), jnp.bfloat16)
    x = panel[held & 127]
    ends = [x[LANES:], none] if k == 0 else [none, x[LANES:]]
    block = jnp.concatenate([pair[pl.ds(k * BS, BS)], pair[pl.ds(2 * BS, BS)]], axis=1)
    product = jnp.dot(block, jnp.concatenate([x[:LANES], *ends], axis=0), preferred_element_type=jnp.float32)
    return lax.shift_right_logical(held, 7), product


def add_pairs(code, first, count, pairs, panel, acc):
    blk = lax.axis_index("blk")

    def step(j, _):
        plane = lax.rem(first + j, 4)
        for u in range(2 * CHUNK):
            at = plane * CHUNK + u // 2
            row, product = pair_product(code, at, blk, u % 2, pairs.at[at], panel)
            acc[row] += product
        return 0

    lax.fori_loop(0, count, step, 0)


def pair_kernel(start, table, pairs, panel, out, acc, code, sem):
    fetch = pltpu.make_async_copy(table, code, sem)
    fetch.start()
    acc[0] = jnp.zeros_like(acc[0])
    acc[1:] = start[...]
    fetch.wait()
    place = Place()
    add_pairs(code, place.zh * 2 + place.zl + 1, 3, pairs, panel, acc)
    out[...] = acc[1:].reshape(out.shape)


def product_kernel(row_of, col_idx, table, vals, pairs, panel, out, vbuf, acc, code, sem, vsem):
    fetch = pltpu.make_async_copy(table, code, sem)
    fetch.start()
    core = lax.rem(lax.axis_index("rep"), 2)
    v_count = vals.shape[0] // (2 * CHUNK)

    def v_copy(j, slot):
        first = (2 * j + core) * CHUNK
        return pltpu.make_async_copy(vals.at[pl.ds(first, CHUNK)], vbuf.at[slot], vsem.at[slot])

    for j in range(DEPTH):
        v_copy(j, j).start()
    acc[...] = jnp.zeros_like(acc)
    fetch.wait()
    add_pairs(code, 0, 4, pairs, panel, acc)

    def v_step(j, _):
        slot = lax.rem(j, DEPTH)
        v_copy(j, slot).wait()
        for u in range(CHUNK):
            s = (2 * j + core) * CHUNK + u
            acc[row_of[s]] += jnp.dot(vbuf[slot, u], panel[col_idx[s]], preferred_element_type=jnp.float32)

        @pl.when(j + DEPTH < v_count)
        def _():
            v_copy(j + DEPTH, slot).start()

        return 0

    lax.fori_loop(0, v_count, v_step, 0)
    out[...] = acc[1:].reshape(out.shape)


def products(row_of, col_idx, table, vals, pairs, g, start=None):
    smem = pl.BlockSpec(memory_space=pltpu.SMEM)
    vmem = pl.BlockSpec(memory_space=pltpu.VMEM)
    hbm = pl.BlockSpec(memory_space=pltpu.HBM)
    work = [
        pltpu.VMEM((5, BS, 2 * LANES), jnp.float32),
        pltpu.SMEM((64, LANES), jnp.int32),
        pltpu.SemaphoreType.DMA,
    ]
    out = pltpu.VMEM((ROWS, 2 * LANES), jnp.float32)
    if start is not None:
        return pl.pallas_call(
            pair_kernel,
            out_shape=out,
            in_specs=[vmem] * 4,
            out_specs=vmem,
            scratch_shapes=work,
            compiler_params=pltpu.CompilerParams(vmem_limit_bytes=4 << 20),
            name="pairs",
        )(start, table, pairs, g)
    return pl.pallas_call(
        product_kernel,
        out_shape=out,
        in_specs=[smem, smem, vmem, hbm, vmem, vmem],
        out_specs=vmem,
        scratch_shapes=[
            pltpu.VMEM((DEPTH, CHUNK, BS, BS), jnp.bfloat16),
            *work,
            pltpu.SemaphoreType.DMA((DEPTH,)),
        ],
        compiler_params=pltpu.CompilerParams(vmem_limit_bytes=12 << 20),
        name="products",
    )(row_of, col_idx, table, vals, pairs, g)


def body(loads, values, row_ptr, col_idx, elem_vals, elem_owner, elem_row, elem_col):
    owners = elem_owner[:, 0]
    count = owners.shape[0]
    order = jnp.arange(count, dtype=jnp.int32)
    earlier = (owners[:, None] == owners[None, :]) & (order[None, :] < order[:, None])
    rank = jnp.sum(earlier.astype(jnp.int32), axis=1)
    slot = owners * 2 + rank
    taken = slot[None, :] == jnp.arange(LANES, dtype=jnp.int32)[:, None]
    places = jnp.sum(jnp.where(taken, order[None, :], 0), axis=1)
    code = jnp.sum(jnp.where(taken, ((elem_row + 1) * 128 + elem_col)[None, :], 0), axis=1)
    codes = jnp.broadcast_to(code[None, :], (8, LANES))
    positions = jnp.arange(values.shape[0], dtype=jnp.int32)
    row = 1 + jnp.sum((positions[:, None] >= row_ptr[0, 1:][None, :]).astype(jnp.int32), axis=1)
    row_of = jnp.where(row > 4, 0, row)
    g, r, table, part = exchange(loads, elem_vals, places, codes, row_of, col_idx, values)

    apply = functools.partial(products, row_of, col_idx, table, values, r)
    part = apply(g, start=part)
    g2 = gather_first(part)
    return sum_cores(apply(g2))


def solution(mesh):
    placed = (
        P("blk", "rep"),
        P("blk", None, None),
        P("blk", None),
        P("blk"),
        P(("blk", "rep"), None, None),
        P(("blk", "rep"), None),
        P(("blk", "rep")),
        P(("blk", "rep")),
    )
    return jax.shard_map(body, mesh=mesh, in_specs=placed, out_specs=P("blk", "rep"), check_vma=False)
```

```python
import functools

import jax
import jax.numpy as jnp
from jax import lax
from jax.experimental import pallas as pl
from jax.experimental.pallas import tpu as pltpu
from jax.sharding import PartitionSpec as P

MESH = pl.DeviceIdType.MESH
BS = 192
ROWS = 768
LANES = 128
HALF = ROWS // 2
PAIR = 3 * BS
CHUNK = 16
DEPTH = 6
GROUP = 3
STORED_ROWS = ((0, 1, (0,)), (1, 2, (0, 1)), (2, 3, (0, 1, 2)), (3, 5, (1, 2, 3)), (5, 7, (2, 3)), (7, 9, (3,)))


class Place:
    def __init__(self):
        blk = lax.axis_index("blk")
        rep = lax.axis_index("rep")
        self.x = lax.rem(blk, 4)
        self.zl = lax.rem(blk // 4, 2)
        self.y = blk // 8
        self.zh = rep // 2
        self.core = lax.rem(rep, 2)

    def block(self, dx, dy, dz):
        x = lax.rem(self.x + dx, 4)
        y = lax.rem(self.y + dy, 4)
        zl = lax.rem(self.zl + dz, 2)
        return (y * 2 + zl) * 4 + x

    def above(self, dz):
        z = lax.rem(self.zh * 2 + self.zl + dz, 4)
        return ((self.y * 2 + lax.rem(z, 2)) * 4 + self.x, (z // 2) * 2 + self.core)

    def device(self, dx, dy, dz, dzh=0, dcore=0):
        zh = lax.rem(self.zh + dzh, 2)
        core = lax.rem(self.core + dcore, 2)
        return (self.block(dx, dy, dz), zh * 2 + core)


SHIFTS = (
    (0, 0), (2, 2), (1, 1), (3, 3), (1, 3), (3, 1), (2, 1), (2, 3),
    (1, 2), (3, 2), (1, 0), (3, 0), (0, 1), (0, 3), (2, 0), (0, 2),
)


def shift(q):
    dx = dy = 0
    for i, (a, b) in enumerate(SHIFTS):
        dx = jnp.where(q == i, a, dx)
        dy = jnp.where(q == i, b, dy)
    return dx, dy


def wait_bytes(ref, sem):
    pltpu.make_async_copy(ref, ref, sem).wait()


class Gather:
    def __init__(self, place, g, late, sems):
        self.place = place
        self.g = g
        self.late = late
        (self.sends, self.cross_s, self.cross_r, self.sem_z, self.sem1, self.sem1f, self.sem2, self.sem2f, self.sem_l) = sems
        self.lanes = pl.ds(pl.multiple_of(place.core * LANES, LANES), LANES)
        self.other = pl.ds(pl.multiple_of((1 - place.core) * LANES, LANES), LANES)

    def peers(self):
        p = self.place
        return [
            p.device(0, 0, 1),
            p.device(1, 0, 0),
            p.device(3, 0, 0),
            p.device(0, 1, 0),
            p.device(0, 3, 0),
            p.device(0, 0, 0, 0, 1),
        ]

    def rows(self, dz):
        return HALF if dz == 0 else HALF - self.late

    def piece(self, half, p1, p2, dz, start=0, size=None):
        block = self.place.block(p1, p2, dz) if half == 0 else self.place.block(p2, p1, dz)
        first = pl.multiple_of(block * ROWS + (half * HALF + start), 64)
        return self.g.at[pl.ds(first, self.rows(dz) if size is None else size), self.lanes]

    def part(self, half, p1, p2, dz, way):
        size = self.rows(dz) // 2
        return self.piece(half, p1, p2, dz, way * size, size)

    def peer(self, half, stage, step):
        along_x = (half == 0) == (stage == 1)
        return self.place.device(step, 0, 0) if along_x else self.place.device(0, step, 0)

    def send(self, ref, device, sem):
        pltpu.make_async_remote_copy(ref, ref, self.sends, sem, device_id=device, device_id_type=MESH).start()

    def cross(self, ref):
        pltpu.make_async_remote_copy(
            ref, ref, self.cross_s, self.cross_r, device_id=self.place.device(0, 0, 0, 0, 1), device_id_type=MESH
        ).start()

    def chunk(self):
        first = pl.multiple_of(self.place.block(0, 0, 0) * ROWS, ROWS)
        return self.g.at[pl.ds(first, ROWS), self.lanes]

    def start(self):
        for half in (0, 1):
            self.send(
                self.piece(half, 0, 0, 0, 0, HALF - self.late), self.place.device(0, 0, 1), self.sem_z.at[half]
            )
        self.spread1(0)
        for half in (0, 1):
            self.spread2(half, 0, 0, 0)
            self.give_late(half, 0, 0)
        self.cross(self.chunk())

    def spread1(self, dz):
        for half in (0, 1):
            for way in (0, 1):
                self.send(
                    self.piece(half, 0, 0, dz), self.peer(half, 1, 1 if way == 0 else 3), self.sem1.at[half, dz, way]
                )

    def spread2(self, half, q, p1, dz):
        for way in (0, 1):
            self.send(
                self.piece(half, p1, 0, dz), self.peer(half, 2, 1 if way == 0 else 3), self.sem2.at[half, q, dz, way]
            )

    def give_late(self, half, p1, p2):
        if self.late:
            self.send(
                self.piece(half, p1, p2, 0, HALF - self.late, self.late),
                self.place.device(0, 0, 1),
                self.sem_l.at[half, p1, p2],
            )

    def take_late(self, p1, p2):
        if self.late:
            for half in (0, 1):
                got = self.piece(half, p1, p2, 1, HALF - self.late, self.late)
                wait_bytes(got, self.sem_l.at[half, p1, p2])
                self.cross(got)

    def neighbour_z(self):
        for half in (0, 1):
            wait_bytes(self.piece(half, 0, 0, 1), self.sem_z.at[half])
        self.spread1(1)
        for half in (0, 1):
            self.spread2(half, 0, 0, 1)
            self.cross(self.piece(half, 0, 0, 1))

    def pass1(self, dz):
        for half in (0, 1):
            for way in (0, 1):
                p1 = 3 if way == 0 else 1
                got = self.piece(half, p1, 0, dz)
                wait_bytes(got, self.sem1.at[half, dz, way])
                self.send(
                    self.part(half, p1, 0, dz, way),
                    self.peer(half, 1, 1 if way == 0 else 3),
                    self.sem1f.at[half, dz, way],
                )
                self.spread2(half, 2 if p1 == 3 else 1, p1, dz)
                self.cross(got)
                if dz == 0:
                    self.give_late(half, p1, 0)

    def far1(self, dz):
        for half in (0, 1):
            for way in (0, 1):
                wait_bytes(self.part(half, 2, 0, dz, way), self.sem1f.at[half, dz, way])
            self.spread2(half, 3, 2, dz)
            self.cross(self.piece(half, 2, 0, dz))
            if dz == 0:
                self.give_late(half, 2, 0)

    def pass2(self, q, dz):
        p1 = q ^ (q // 2)
        for half in (0, 1):
            for way in (0, 1):
                p2 = 3 if way == 0 else 1
                got = self.piece(half, p1, p2, dz)
                wait_bytes(got, self.sem2.at[half, q, dz, way])
                self.send(
                    self.part(half, p1, p2, dz, way),
                    self.peer(half, 2, 1 if way == 0 else 3),
                    self.sem2f.at[half, q, dz, way],
                )
                self.cross(got)
                if dz == 0:
                    self.give_late(half, p1, p2)

    def far2(self, q, dz):
        p1 = q ^ (q // 2)
        for half in (0, 1):
            for way in (0, 1):
                wait_bytes(self.part(half, p1, 2, dz, way), self.sem2f.at[half, q, dz, way])
            self.cross(self.piece(half, p1, 2, dz))
            if dz == 0:
                self.give_late(half, p1, 2)

    def finish(self):
        wait_bytes(self.g.at[:, self.other], self.cross_r)
        wait_bytes(self.g.at[:, self.lanes], self.cross_s)
        wait_bytes(self.g.at[pl.ds(0, 31 * ROWS), self.lanes], self.sends)


def gather_scratch():
    dma = pltpu.SemaphoreType.DMA
    return [
        dma,
        dma,
        dma,
        dma((2,)),
        dma((2, 2, 2)),
        dma((2, 2, 2)),
        dma((2, 4, 2, 2)),
        dma((2, 4, 2, 2)),
        dma((2, 4, 4)),
    ]


def greet(devices):
    barrier = pltpu.get_barrier_semaphore()
    for device in devices:
        pl.semaphore_signal(barrier, inc=1, device_id=device, device_id_type=MESH)
    return barrier


def exchange_kernel(loads, elems, places, codes, row_of, col_idx, vals, g, r, table, part, m, near, v, t, held, packed, ed, es, er, ee, eo, ms, mz, mr, mzr, own, hsem, vsem, nsem, *sems):
    place = Place()
    r = r.reshape(4, 16, PAIR, LANES)
    gather = Gather(place, g.reshape(32 * ROWS, 2 * LANES), 0, sems)
    spot = place.y * 4 + place.x
    me = place.block(0, 0, 0)
    level = place.zh * 2 + place.zl
    barrier = greet(gather.peers() + [place.above(dz) for dz in (1, 2, 3)])

    def greet_step(q, _):
        dx, dy = shift(q)
        pl.semaphore_signal(barrier, inc=1, device_id=place.device(dx, dy, 0), device_id_type=MESH)
        return 0

    lax.fori_loop(1, 16, greet_step, 0)
    mine = pltpu.make_async_copy(loads, gather.chunk(), own)
    mine.start()
    holding = pltpu.make_async_copy(elems, held, hsem)
    holding.start()

    def fetch(j, _):
        first = (2 * j + place.core) * CHUNK
        pltpu.make_async_copy(vals.at[pl.ds(first, CHUNK)], v.at[pl.ds(j * CHUNK, CHUNK)], vsem).start()
        return 0

    lax.fori_loop(0, v.shape[0] // CHUNK, fetch, 0)

    mine.wait()
    pl.semaphore_wait(barrier, 6 + 3 + 15)

    def send(source, target, send_sem, recv_sem, device):
        pltpu.make_async_remote_copy(
            source, target, send_sem, recv_sem, device_id=device, device_id_type=MESH
        ).start()

    def pack(q, dx, dy):
        for dz in (0, 1):
            target = place.block(dx, dy, dz)
            one = held[places[target * 2]]
            two = held[places[target * 2 + 1]]
            packed[q, dz, pl.ds(0, BS), :] = one[:, :LANES]
            packed[q, dz, pl.ds(BS, BS), :] = two[:, :LANES]
            packed[q, dz, pl.ds(2 * BS, BS), :] = jnp.concatenate([one[:, LANES:], two[:, LANES:]], axis=1)

    def hand_on(mine, others, at):
        send(mine, r.at[level, at], es, er, place.above(2))
        send(others, r.at[level, at], es, er, place.above(1))
        send(others, r.at[level, at], es, er, place.above(3))

    def elements(q):
        dx, dy = shift(q)
        pack(q, dx, dy)
        device = place.device(dx, dy, 0)
        send(packed.at[q, 0], r.at[level, spot], ed, ee.at[q], device)
        send(packed.at[q, 1], t.at[spot], ed, eo.at[q], device)
        send(codes, m.at[level, spot], ms, mr, device)

    def own_elements():
        pack(0, 0, 0)
        hand_on(packed.at[0, 0], packed.at[0, 1], spot)
        pltpu.make_async_copy(packed.at[0, 0], r.at[level, spot], ee.at[0]).start()
        pltpu.make_async_copy(packed.at[0, 1], t.at[spot], eo.at[0]).start()
        pltpu.make_async_copy(codes, m.at[level, spot], mr).start()

    def relay(q):
        dx, dy = shift(q)
        at = lax.rem(place.y + 4 - dy, 4) * 4 + lax.rem(place.x + 4 - dx, 4)
        wait_bytes(r.at[level, at], ee.at[q])
        wait_bytes(t.at[at], eo.at[q])
        hand_on(r.at[level, at], t.at[at], at)

    def loop(first, last, step):
        def one(k, _):
            step(k)
            return 0

        lax.fori_loop(first, last, one, 0)

    holding.wait()
    own_elements()
    loop(1, 16, elements)
    gather.start()
    loop(1, 16, relay)
    gather.pass1(0)
    gather.neighbour_z()
    gather.far1(0)
    loop(0, 3, lambda q: gather.pass2(q, 0))
    gather.pass1(1)
    loop(3, 4, lambda q: gather.pass2(q, 0))
    gather.far1(1)
    loop(0, 4, lambda q: gather.far2(q, 0))
    loop(0, 4, lambda q: gather.pass2(q, 1))
    loop(0, 4, lambda q: gather.far2(q, 1))
    wait_bytes(r.at[level, spot], ee.at[0])
    wait_bytes(t.at[spot], eo.at[0])
    wait_bytes(m.at[level], mr)
    for dz in (1, 2, 3):
        send(m.at[level], m.at[level], mz, mzr, place.above(dz))
    part[...] = jnp.zeros_like(part)
    wait_bytes(v, vsem)
    gather.finish()
    for first, last, rows in STORED_ROWS:

        def stored(j):
            for u in range(CHUNK):
                s = (2 * j + place.core) * CHUNK + u
                product = jnp.dot(v[j * CHUNK + u], g[col_idx[s]], preferred_element_type=jnp.float32)
                row = row_of[s]
                for i in rows:
                    part[i] += jnp.where(row == i + 1, product, 0.0)

        loop(first, last, stored)
    here = pl.ds(pl.multiple_of(level * 16, 16), 16)
    table[here, :] = m[level, :, 0, :]
    pltpu.make_async_copy(table.at[here], near, nsem).start()
    wait_bytes(near, nsem)

    def arrived(j):
        for u in range(CHUNK):
            at = j * (CHUNK // 2) + u // 2
            row, product = pair_product(near, at, me, u % 2, r.at[level, at], g)
            for i in range(4):
                part[i] += jnp.where(row == i + 1, product, 0.0)

    loop(0, 2, arrived)
    wait_bytes(r.at[pl.ds(0, 3)], er)
    wait_bytes(m.at[pl.ds(0, 3)], mzr)
    wait_bytes(r.at[pl.ds(0, 3)], es)
    wait_bytes(packed.at[pl.ds(0, 15)], ed)
    wait_bytes(m.at[0, pl.ds(0, 15)], ms)
    wait_bytes(m.at[pl.ds(0, 3)], mz)
    table[...] = m[:, :, 0, :].reshape(64, LANES)


def exchange(loads, elems, places, codes, row_of, col_idx, vals):
    hbm = pl.BlockSpec(memory_space=pltpu.HBM)
    vmem = pl.BlockSpec(memory_space=pltpu.VMEM)
    dma = pltpu.SemaphoreType.DMA
    return pl.pallas_call(
        exchange_kernel,
        out_shape=[
            pltpu.VMEM((128, BS, 2 * LANES), jnp.bfloat16),
            pltpu.VMEM((64, PAIR, LANES), jnp.bfloat16),
            pltpu.VMEM((64, LANES), jnp.int32),
            pltpu.VMEM((4, BS, 2 * LANES), jnp.float32),
        ],
        in_specs=[
            hbm,
            hbm,
            pl.BlockSpec(memory_space=pltpu.SMEM),
            hbm,
            pl.BlockSpec(memory_space=pltpu.SMEM),
            pl.BlockSpec(memory_space=pltpu.SMEM),
            hbm,
        ],
        out_specs=[vmem] * 4,
        scratch_shapes=[
            pltpu.VMEM((4, 16, 8, LANES), jnp.int32),
            pltpu.SMEM((16, LANES), jnp.int32),
            pltpu.VMEM((vals.shape[0] // 2, BS, BS), jnp.bfloat16),
            pltpu.VMEM((16, PAIR, LANES), jnp.bfloat16),
            pltpu.VMEM(elems.shape, jnp.bfloat16),
            pltpu.VMEM((16, 2, PAIR, LANES), jnp.bfloat16),
            dma,
            dma,
            dma,
            dma((16,)),
            dma((16,)),
            dma,
            dma,
            dma,
            dma,
            dma,
            dma,
            dma,
            dma,
            *gather_scratch(),
        ],
        compiler_params=pltpu.CompilerParams(collective_id=1, has_side_effects=True, vmem_limit_bytes=30 << 20),
        name="exchange",
    )(loads, elems, places, codes, row_of, col_idx, vals)


def share_sum(place, part, came, send_sem, recv_sem):
    lanes = pl.ds(pl.multiple_of(place.core * LANES, LANES), LANES)
    other = pl.ds(pl.multiple_of((1 - place.core) * LANES, LANES), LANES)
    copy = pltpu.make_async_remote_copy(
        part.at[:, other], came, send_sem, recv_sem, device_id=place.device(0, 0, 0, 0, 1), device_id_type=MESH
    )
    copy.start()
    copy.wait()
    return part[:, lanes] + came[...]


def gather_kernel(part, g, came, send_sem, recv_sem, *sems):
    place = Place()
    gather = Gather(place, g.reshape(32 * ROWS, 2 * LANES), 128, sems)
    barrier = greet(gather.peers())
    pl.semaphore_wait(barrier, 6)
    gather.chunk()[...] = share_sum(place, part, came, send_sem, recv_sem).astype(jnp.bfloat16)
    gather.start()
    gather.pass1(0)
    gather.neighbour_z()
    gather.far1(0)

    def loop(first, last, step):
        def one(q, _):
            step(q)
            return 0

        lax.fori_loop(first, last, one, 0)

    loop(0, 3, lambda q: gather.pass2(q, 0))
    gather.pass1(1)
    loop(3, 4, lambda q: gather.pass2(q, 0))
    gather.far1(1)
    loop(0, 4, lambda q: gather.far2(q, 0))

    def step2(q):
        gather.pass2(q, 1)
        gather.take_late(q, 0)

    loop(0, 4, step2)

    def step3(q):
        gather.far2(q, 1)
        gather.take_late(q, 1)
        gather.take_late(q, 3)

    loop(0, 4, step3)
    loop(0, 4, lambda q: gather.take_late(q, 2))
    gather.finish()


def gather_first(part):
    dma = pltpu.SemaphoreType.DMA
    return pl.pallas_call(
        gather_kernel,
        out_shape=pltpu.VMEM((128, BS, 2 * LANES), jnp.bfloat16),
        in_specs=[pl.BlockSpec(memory_space=pltpu.VMEM)],
        out_specs=pl.BlockSpec(memory_space=pltpu.VMEM),
        scratch_shapes=[
            pltpu.VMEM((ROWS, LANES), jnp.float32),
            dma,
            dma,
            *gather_scratch(),
        ],
        compiler_params=pltpu.CompilerParams(collective_id=2, has_side_effects=True, vmem_limit_bytes=4 << 20),
        name="gather_first",
    )(part)


def sum_kernel(part, out, came, send_sem, recv_sem):
    place = Place()
    barrier = greet([place.device(0, 0, 0, 0, 1)])
    pl.semaphore_wait(barrier, 1)
    out[...] = share_sum(place, part, came, send_sem, recv_sem)


def sum_cores(part):
    dma = pltpu.SemaphoreType.DMA
    return pl.pallas_call(
        sum_kernel,
        out_shape=jax.ShapeDtypeStruct((ROWS, LANES), jnp.float32),
        in_specs=[pl.BlockSpec(memory_space=pltpu.VMEM)],
        out_specs=pl.BlockSpec(memory_space=pltpu.VMEM),
        scratch_shapes=[pltpu.VMEM((ROWS, LANES), jnp.float32), dma, dma],
        compiler_params=pltpu.CompilerParams(collective_id=3, has_side_effects=True, vmem_limit_bytes=4 << 20),
        name="sum_cores",
    )(part)


def pair_product(code, at, blk, k, pair, panel):
    held = code[at, blk * 2 + k]
    none = jnp.zeros((64, 2 * LANES), jnp.bfloat16)
    x = panel[held & 127]
    ends = [x[LANES:], none] if k == 0 else [none, x[LANES:]]
    block = jnp.concatenate([pair[pl.ds(k * BS, BS)], pair[pl.ds(2 * BS, BS)]], axis=1)
    product = jnp.dot(block, jnp.concatenate([x[:LANES], *ends], axis=0), preferred_element_type=jnp.float32)
    return lax.shift_right_logical(held, 7), product


def add_pairs(code, first, count, pairs, panel, acc):
    blk = lax.axis_index("blk")

    def step(j, _):
        plane = lax.rem(first + j, 4)
        for u in range(2 * CHUNK):
            at = plane * CHUNK + u // 2
            row, product = pair_product(code, at, blk, u % 2, pairs.at[at], panel)
            acc[row] += product
        return 0

    lax.fori_loop(0, count, step, 0)


def pair_kernel(start, table, pairs, panel, out, acc, code, sem):
    fetch = pltpu.make_async_copy(table, code, sem)
    fetch.start()
    acc[0] = jnp.zeros_like(acc[0])
    acc[1:] = start[...]
    fetch.wait()
    place = Place()
    add_pairs(code, place.zh * 2 + place.zl + 1, 3, pairs, panel, acc)
    out[...] = acc[1:].reshape(out.shape)


def product_kernel(row_of, col_idx, table, vals, pairs, panel, out, vbuf, acc, code, sem, vsem):
    fetch = pltpu.make_async_copy(table, code, sem)
    fetch.start()
    core = lax.rem(lax.axis_index("rep"), 2)
    v_count = vals.shape[0] // (2 * CHUNK)

    def v_copy(j, slot):
        first = (2 * j + core) * CHUNK
        return pltpu.make_async_copy(vals.at[pl.ds(first, CHUNK)], vbuf.at[slot], vsem.at[slot])

    for j in range(DEPTH):
        v_copy(j, j).start()
    acc[...] = jnp.zeros_like(acc)
    fetch.wait()
    add_pairs(code, 0, 4, pairs, panel, acc)

    def v_step(group, _):
        for i in range(GROUP):
            v_copy(group * GROUP + i, lax.rem(group * GROUP + i, DEPTH)).wait()
        for i in range(GROUP):
            j = group * GROUP + i
            slot = lax.rem(j, DEPTH)
            for u in range(CHUNK):
                s = (2 * j + core) * CHUNK + u
                acc[row_of[s]] += jnp.dot(vbuf[slot, u], panel[col_idx[s]], preferred_element_type=jnp.float32)

        @pl.when((group + 1) * GROUP + DEPTH - GROUP < v_count)
        def _():
            for i in range(GROUP):
                j = group * GROUP + i
                v_copy(j + DEPTH, lax.rem(j, DEPTH)).start()

        return 0

    lax.fori_loop(0, v_count // GROUP, v_step, 0)
    out[...] = acc[1:].reshape(out.shape)


def products(row_of, col_idx, table, vals, pairs, g, start=None):
    smem = pl.BlockSpec(memory_space=pltpu.SMEM)
    vmem = pl.BlockSpec(memory_space=pltpu.VMEM)
    hbm = pl.BlockSpec(memory_space=pltpu.HBM)
    work = [
        pltpu.VMEM((5, BS, 2 * LANES), jnp.float32),
        pltpu.SMEM((64, LANES), jnp.int32),
        pltpu.SemaphoreType.DMA,
    ]
    out = pltpu.VMEM((ROWS, 2 * LANES), jnp.float32)
    if start is not None:
        return pl.pallas_call(
            pair_kernel,
            out_shape=out,
            in_specs=[vmem] * 4,
            out_specs=vmem,
            scratch_shapes=work,
            compiler_params=pltpu.CompilerParams(vmem_limit_bytes=4 << 20),
            name="pairs",
        )(start, table, pairs, g)
    return pl.pallas_call(
        product_kernel,
        out_shape=out,
        in_specs=[smem, smem, vmem, hbm, vmem, vmem],
        out_specs=vmem,
        scratch_shapes=[
            pltpu.VMEM((DEPTH, CHUNK, BS, BS), jnp.bfloat16),
            *work,
            pltpu.SemaphoreType.DMA((DEPTH,)),
        ],
        compiler_params=pltpu.CompilerParams(vmem_limit_bytes=14 << 20),
        name="products",
    )(row_of, col_idx, table, vals, pairs, g)


def body(loads, values, row_ptr, col_idx, elem_vals, elem_owner, elem_row, elem_col):
    owners = elem_owner[:, 0]
    count = owners.shape[0]
    order = jnp.arange(count, dtype=jnp.int32)
    earlier = (owners[:, None] == owners[None, :]) & (order[None, :] < order[:, None])
    rank = jnp.sum(earlier.astype(jnp.int32), axis=1)
    slot = owners * 2 + rank
    taken = slot[None, :] == jnp.arange(LANES, dtype=jnp.int32)[:, None]
    places = jnp.sum(jnp.where(taken, order[None, :], 0), axis=1)
    code = jnp.sum(jnp.where(taken, ((elem_row + 1) * 128 + elem_col)[None, :], 0), axis=1)
    codes = jnp.broadcast_to(code[None, :], (8, LANES))
    positions = jnp.arange(values.shape[0], dtype=jnp.int32)
    row = 1 + jnp.sum((positions[:, None] >= row_ptr[0, 1:][None, :]).astype(jnp.int32), axis=1)
    row_of = jnp.where(row > 4, 0, row)
    g, r, table, part = exchange(loads, elem_vals, places, codes, row_of, col_idx, values)

    apply = functools.partial(products, row_of, col_idx, table, values, r)
    part = apply(g, start=part)
    g2 = gather_first(part)
    return sum_cores(apply(g2))


def solution(mesh):
    placed = (
        P("blk", "rep"),
        P("blk", None, None),
        P("blk", None),
        P("blk"),
        P(("blk", "rep"), None, None),
        P(("blk", "rep"), None),
        P(("blk", "rep")),
        P(("blk", "rep")),
    )
    return jax.shard_map(body, mesh=mesh, in_specs=placed, out_specs=P("blk", "rep"), check_vma=False)
```
